256 devices in a mesh: gx: 16 (over y, x), gy: 16 (over z, core).
Axes of the slice: x: 4, y: 4, z: 8, core: 2. Of those that a mesh axis runs over, the one named last changes fastest.
Arguments:
- tree_order: int32 [256, 4096], P(('gy', 'gx')), may hold values from 0 to 4095, each once within a row
- targets: float32 [1048576, 128], P(('gy', 'gx')), may hold values from -6 to 6
- noise_var: float32 [1048576], P(('gy', 'gx')), may hold values from 0.5 to 2
- node_bases: float32 [4, 1048576, 128], P(None, ('gy', 'gx')), may hold values from -6 to 6
Outputs:
- solved: float32 [1048576, 128], P(('gy', 'gx'))
- node_weights: float32 [64, 128, 128], P('gy')
The draws below stay inside these ranges and needn't reach their ends.
Inputs may be any that keep to these rules, and one draw needn't show every extreme that they name: Each row of tree_order is a permutation of 0 to 4095.
All inputs are finite; a program needn't handle non-finite values.
Results may differ from the reference program's by a relative error of at most 0.0001.
Values sent between devices are 32-bit elements; how exact they have to be, the bound alone decides.
No kernel may reach another device: no remote copies, remote signals or barrier semaphores. Data moves between devices by JAX's collectives and lax.ppermute only.
A program may use at most 128 MiB of HBM per device.

```python
import math
import jax
import jax.numpy as jnp
from jax import lax

PTS_DEV = 4096
RANK = 128
PROBES = 128
LEVELS = 4
BLOCKS = 256
POINTS = 1048576
N_GY = 16


def level_of(rng, dims, shards, smallest, high):
    level = 1.0
    for position, blocks in shards:
        draws = jax.random.uniform(jax.random.fold_in(jax.random.fold_in(rng, 6), position), (blocks,), jnp.float32, smallest / len(shards), high / len(shards))
        level = level * jnp.repeat(jnp.exp(draws), dims[position] // blocks).reshape((-1,) + (1,) * (len(dims) - 1 - position))
    return level


def centred(key, dims, spread, limit, split=(), held_as=jnp.bfloat16):
    level = level_of(key, dims, split, -0.22, 0.18) if split else 1.0
    values = jax.random.normal(key, dims, jnp.float32) * spread * level
    return jnp.minimum(jnp.maximum(values, -limit), limit).astype(held_as)


def setup_inputs(seed: int = 0) -> dict:
    key_of = jax.random.split(jax.random.key(seed), 5)
    return {
        "tree_order": jax.vmap(lambda own: jax.random.permutation(own, PTS_DEV))(jax.random.split(key_of[0], BLOCKS)).reshape((BLOCKS, PTS_DEV)).astype(jnp.int32),
        "targets": centred(key_of[1], (POINTS, PROBES), 1.0, 6.0, ((0, 256),), jnp.float32),
        "noise_var": jnp.clip(jnp.exp(math.log(2.0) - 1.3862944 * jax.random.uniform(key_of[2], (POINTS,), jnp.float32) ** level_of(key_of[2], (POINTS,), ((0, 256),), -0.2, 0.2)), 0.5, 2.0),
        "node_bases": centred(key_of[3], (LEVELS, POINTS, RANK), 1.0, 6.0, ((1, 256),), jnp.float32),
    }


def chol_apply(factor, rhs):
    first = lax.linalg.triangular_solve(factor, rhs, left_side=True, lower=True)
    return lax.linalg.triangular_solve(factor, first, left_side=True, lower=True, transpose_a=True)

def reference(tree_order, targets, noise_var, node_bases):
    blocks = tree_order.shape[0]
    points_here = tree_order.shape[1]
    local_targets = targets.reshape(blocks, points_here, PROBES)
    tree_targets = jnp.take_along_axis(local_targets, tree_order[:, :, None].astype(jnp.int32), axis=1)
    inverse_noise = (1.0 / noise_var).reshape(blocks, points_here, 1)
    solved_b = tree_targets * inverse_noise
    scaled = [node_bases[tree_level].reshape(blocks, points_here, RANK) * (POINTS / 2 ** tree_level) ** (-0.5) for tree_level in range(LEVELS)]
    solved_v = [basis_rows * inverse_noise for basis_rows in scaled]
    weights_found = [None] * LEVELS
    for tree_level in range(LEVELS - 1, -1, -1):
        node_count = 2 ** tree_level
        remaining = jnp.concatenate([solved_b] + solved_v[:tree_level], axis=2)
        width_rest = remaining.shape[2]
        own_cols = solved_v[tree_level]
        basis_rows = scaled[tree_level].reshape(node_count, -1, RANK)
        gram_rest = jnp.einsum('nmr,nmc->nrc', basis_rows, remaining.reshape(node_count, -1, width_rest), precision=lax.Precision.HIGHEST)
        gram_own = jnp.einsum('nmr,nmc->nrc', basis_rows, own_cols.reshape(node_count, -1, RANK), precision=lax.Precision.HIGHEST)
        capacitance = jnp.eye(RANK, dtype=jnp.float32)[None] + 0.5 * (gram_own + jnp.swapaxes(gram_own, 1, 2))
        factor = jnp.linalg.cholesky(capacitance)
        coefficients = chol_apply(factor, gram_rest)
        block_coefs = jnp.repeat(coefficients, blocks // node_count, axis=0)
        remaining = remaining - jnp.einsum('bpr,brc->bpc', own_cols, block_coefs, precision=lax.Precision.HIGHEST)
        solved_b = remaining[:, :, :PROBES]
        for lower in range(tree_level):
            solved_v[lower] = remaining[:, :, PROBES + lower * RANK:PROBES + (lower + 1) * RANK]
        weights_found[tree_level] = jnp.repeat(coefficients[:, :, :PROBES], N_GY // node_count, axis=0)
    node_weights = jnp.stack(weights_found, axis=1).reshape(LEVELS * N_GY, RANK, PROBES)
    row_index = jnp.arange(blocks, dtype=jnp.int32)[:, None]
    solved = jnp.zeros_like(solved_b).at[row_index, tree_order.astype(jnp.int32)].set(solved_b)
    return (solved.reshape(POINTS, PROBES), node_weights)
```

```python
import functools

import jax
import jax.numpy as jnp
from jax import lax
from jax.experimental import pallas as pl
from jax.experimental.pallas import tpu as pltpu
from jax.sharding import Mesh, PartitionSpec as P

R = 128
TILE = 1024
F32 = jnp.float32
BF16 = jnp.bfloat16
VMEM_LIMIT = 56 * 1024 * 1024


def three(a):
    a1 = a.astype(BF16)
    rest = a - a1.astype(F32)
    a2 = rest.astype(BF16)
    return a1, a2, (rest - a2.astype(F32)).astype(BF16)


def left3(a):
    a1, a2 = split(a)
    return jnp.concatenate([a1, a1, a2], axis=1)


def right3(b):
    b1, b2 = split(b)
    return jnp.concatenate([b1, b2, b1], axis=0)


def left6(a):
    a1, a2, a3 = three(a)
    return jnp.concatenate([a1, a1, a2, a1, a3, a2], axis=1)


def right6(b):
    b1, b2, b3 = three(b)
    return jnp.concatenate([b1, b2, b1, b3, b1, b2], axis=0)


def dot3(a, b):
    return dot16(left3(a), right3(b))


def dot(a, b):
    return dot16(left6(a), right6(b))


def dot16(a, b):
    return jnp.dot(a, b, preferred_element_type=F32)


def dot16_t(a, b):
    return lax.dot_general(a, b, (((0,), (0,)), ((), ())), preferred_element_type=F32)


def split(a):
    high = a.astype(BF16)
    return high, (a - high.astype(F32)).astype(BF16)


def column(rows):
    parts = [
        jnp.broadcast_to(rows[i : i + 1, :], (R, R)).T for i in range(rows.shape[0])
    ]
    return jnp.concatenate(parts, axis=0)


def block(i):
    return pl.ds(i * R, R)


def block_list(levels):
    return [(k, c) for k in range(levels - 1, -1, -1) for c in range(-1, k + 1)]


def gram_kernel(levels, scales, order, core, targets, noise, bases,
                gathered, keep, give, acc, acc_t, whole):
    step = pl.program_id(0)
    tile = bases.shape[1]
    width = levels * R

    @pl.when(step == 0)
    def _():
        acc[...] = jnp.zeros_like(acc)
        acc_t[...] = jnp.zeros_like(acc_t)

    for row in range(tile):
        gathered[pl.ds(row, 1), :] = targets[pl.ds(order[step * tile + row], 1), :]
    root = column(1.0 / jnp.sqrt(noise[pl.ds(step * (tile // R), tile // R), :]))
    pieces = [split(bases[k] * root) for k in range(levels)]
    high = jnp.concatenate([p[0] for p in pieces], axis=1)
    low = jnp.concatenate([p[1] for p in pieces], axis=1)
    right_h, right_l = split(gathered[...] * root)
    turned = high.T
    every = jnp.concatenate([high, low, right_h, right_l], axis=1)
    near = width // 2
    acc[0:near, 0:near] += dot16(turned[0:near, :], high[:, 0:near])
    acc[:, near:] += dot16(turned, every[:, near:])
    acc_t[...] += dot16(right_h.T, low)

    @pl.when(step == pl.num_programs(0) - 1)
    def _():
        blocks = block_list(levels)
        half = len(blocks) // 2
        for at, (k, c) in enumerate(blocks):
            rows = block(k)
            if c < 0:
                value = (
                    acc[rows, block(2 * levels)]
                    + acc[rows, block(2 * levels + 1)]
                    + acc_t[:, block(k)].T
                ) * scales[k]
            else:
                same = acc[rows, block(c)]
                if c < levels // 2 <= k:
                    same = acc[block(c), rows].T
                value = (
                    same
                    + acc[rows, block(levels + c)]
                    + acc[block(c), block(levels + k)].T
                ) * (scales[k] * scales[c])
            whole[block(at), :] = value
        rows = half * R

        @pl.when(core[0] == 0)
        def _():
            keep[...] = whole[0:rows, :]
            give[...] = whole[rows : 2 * rows, :]

        @pl.when(core[0] != 0)
        def _():
            give[...] = whole[0:rows, :]
            keep[...] = whole[rows : 2 * rows, :]


def grams(order, core, targets, noise, bases, scales):
    levels, points, _ = bases.shape
    half = len(block_list(levels)) // 2 * R
    width = levels * R
    grid_spec = pltpu.PrefetchScalarGridSpec(
        num_scalar_prefetch=2,
        grid=(points // TILE,),
        in_specs=[
            pl.BlockSpec((points, R), lambda i, *_: (0, 0)),
            pl.BlockSpec((points // R, R), lambda i, *_: (0, 0)),
            pl.BlockSpec((levels, TILE, R), lambda i, *_: (0, i, 0)),
        ],
        out_specs=[
            pl.BlockSpec((TILE, R), lambda i, *_: (i, 0)),
            pl.BlockSpec((half, R), lambda i, *_: (0, 0)),
            pl.BlockSpec((half, R), lambda i, *_: (0, 0)),
        ],
        scratch_shapes=[
            pltpu.VMEM((width, 2 * width + 2 * R), F32),
            pltpu.VMEM((R, width), F32),
            pltpu.VMEM((2 * half, R), F32),
        ],
    )
    return pl.pallas_call(
        functools.partial(gram_kernel, levels, scales),
        grid_spec=grid_spec,
        out_shape=[
            jax.ShapeDtypeStruct((points, R), F32),
            jax.ShapeDtypeStruct((half, R), F32),
            jax.ShapeDtypeStruct((half, R), F32),
        ],
        compiler_params=pltpu.CompilerParams(vmem_limit_bytes=VMEM_LIMIT),
        name="grams",
    )(order, core, targets, noise, bases)


def sum_kernel(copies, parts, out):
    total = parts[0]
    for i in range(1, parts.shape[0]):
        total = total + parts[i]
    for i in range(copies):
        out[i] = total


def sum_and_copy(parts):
    return pl.pallas_call(
        functools.partial(sum_kernel, parts.shape[0]),
        out_shape=jax.ShapeDtypeStruct(parts.shape, F32),
        name="sum_parts",
    )(parts)


def inverse(c, power, result):
    n = c.shape[0]
    on_diagonal = lax.broadcasted_iota(jnp.int32, (n, n), 0) == lax.broadcasted_iota(
        jnp.int32, (n, n), 1
    )
    eye = jnp.where(on_diagonal, 1.0, 0.0).astype(F32)
    diagonal = jnp.sum(c * eye, axis=0, keepdims=True)
    radius = jnp.sum(jnp.abs(c), axis=0, keepdims=True) - jnp.abs(diagonal)
    top = jnp.max(diagonal + radius)
    low = jnp.maximum(jnp.min(diagonal - radius), 1.0)
    factor = 2.0 / (low + top)
    bound = (top - low) / (low + top)
    power[...] = eye - factor * c
    result[...] = factor * (eye + power[...])

    def cond(bound):
        return bound > 1e-4

    def body(bound):
        e = dot3(power[...], power[...])
        power[...] = e
        result[...] += dot3(result[...], e)
        return bound * bound

    lax.while_loop(cond, body, bound * bound)

    def cond_r(state):
        return jnp.logical_and(state[0] > 1e-4, state[1] < 8)

    def body_r(state):
        x = result[...]
        residual = eye - dot(c, x)
        result[...] = x + dot3(x, residual)
        return jnp.max(jnp.abs(residual)), state[1] + 1

    lax.while_loop(cond_r, body_r, (jnp.float32(1.0), jnp.int32(0)))
    return result[...]


def eliminate(level, total, weights, rest, power, result):
    n = R
    own = total[block(level + 1), :]
    on_diagonal = lax.broadcasted_iota(jnp.int32, (n, n), 0) == lax.broadcasted_iota(
        jnp.int32, (n, n), 1
    )
    c = jnp.where(on_diagonal, 1.0, 0.0).astype(F32) + 0.5 * (own + own.T)
    inv = inverse(c, power, result)
    found = []
    inv = left6(inv)
    for i in range(level + 1):
        value = dot16(inv, right6(total[block(i), :]))
        weights[i] = value
        found.append(right6(value))
    at = 0
    for k in range(level - 1, -1, -1):
        left = left6(total[block(k + 1), :].T)
        for col in range(-1, k + 1):
            old = total[block(level + 2 + at), :]
            rest(at, old - dot16(left, found[col + 1]))
            at += 1


def level_kernel(level, first, core, *refs):
    if first:
        mine, other, weights, left, give, total, power, result = refs
        half = mine.shape[0]

        @pl.when(core[0] == 0)
        def _():
            total[0:half, :] = mine[...]
            total[half : 2 * half, :] = other[...]

        @pl.when(core[0] != 0)
        def _():
            total[0:half, :] = other[...]
            total[half : 2 * half, :] = mine[...]
    else:
        before, mine, other, weights, left, give, total, power, result = refs
        half = mine.shape[0]

        @pl.when(core[0] == 0)
        def _():
            total[0:half, :] = before[0:half, :] + mine[...]
            total[half : 2 * half, :] = before[half : 2 * half, :] + other[...]

        @pl.when(core[0] != 0)
        def _():
            total[0:half, :] = before[0:half, :] + other[...]
            total[half : 2 * half, :] = before[half : 2 * half, :] + mine[...]

    def put(at, value):
        left[block(at), :] = value

    eliminate(level, total, weights, put, power, result)
    size = give.shape[0]

    @pl.when(core[0] == 0)
    def _():
        give[...] = left[0:size, :]

    @pl.when(core[0] != 0)
    def _():
        give[...] = left[size : 2 * size, :]


def solve_level(level, core, incoming):
    first = len(incoming) == 2
    rows = 2 * incoming[-1].shape[0]
    after = len(block_list(level)) * R
    smem = pl.BlockSpec(memory_space=pltpu.SMEM)
    vmem = pl.BlockSpec(memory_space=pltpu.VMEM)
    return pl.pallas_call(
        functools.partial(level_kernel, level, first),
        in_specs=[smem] + [vmem] * len(incoming),
        out_specs=[vmem] * 3,
        out_shape=[
            jax.ShapeDtypeStruct((level + 1, R, R), F32),
            jax.ShapeDtypeStruct((after, R), F32),
            jax.ShapeDtypeStruct((after // 2, R), F32),
        ],
        scratch_shapes=[pltpu.VMEM((rows, R), F32)] + [pltpu.VMEM((R, R), F32)] * 2,
        compiler_params=pltpu.CompilerParams(vmem_limit_bytes=VMEM_LIMIT),
        name="level",
    )(core, *incoming)


def apply_kernel(levels, scales, order, core, before, mine, other, *refs):
    weights = refs[: levels - 1]
    noise, bases, gathered, solved, node_weights, total, coefs_h, coefs_l, held, power, result = refs[levels - 1 :]
    step = pl.program_id(0)
    tile = bases.shape[1]

    @pl.when(step == 0)
    def _():
        half = mine.shape[0]

        @pl.when(core[0] == 0)
        def _():
            total[0:half, :] = before[0:half, :] + mine[...]
            total[half : 2 * half, :] = before[half : 2 * half, :] + other[...]

        @pl.when(core[0] != 0)
        def _():
            total[0:half, :] = before[0:half, :] + other[...]
            total[half : 2 * half, :] = before[half : 2 * half, :] + mine[...]

        own = total[block(1), :]
        on_diagonal = lax.broadcasted_iota(jnp.int32, (R, R), 0) == lax.broadcasted_iota(
            jnp.int32, (R, R), 1
        )
        c = jnp.where(on_diagonal, 1.0, 0.0).astype(F32) + 0.5 * (own + own.T)
        found = [dot(inverse(c, power, result), total[block(0), :])]
        node_weights[0] = found[0]
        for k in range(1, levels):
            w = weights[k - 1]
            value = w[0]
            node_weights[k] = value
            for j in range(k):
                value = value - dot(w[j + 1], found[j])
            found.append(value)
        for k in range(levels):
            high, low = split(found[k] * scales[k])
            coefs_h[block(k), :] = high
            coefs_l[block(k), :] = low

    inverse_noise = column(1.0 / noise[pl.ds(step * (tile // R), tile // R), :])
    pieces = [split(bases[k]) for k in range(levels)]
    high = jnp.concatenate([p[0] for p in pieces], axis=1)
    low = jnp.concatenate([p[1] for p in pieces], axis=1)
    change = dot16(high, coefs_h[...]) + (dot16(high, coefs_l[...]) + dot16(low, coefs_h[...]))
    held[...] = (gathered[...] - change) * inverse_noise
    for row in range(tile):
        solved[pl.ds(order[step * tile + row], 1), :] = held[pl.ds(row, 1), :]


def apply(order, core, incoming, weights, noise, bases, gathered, scales):
    levels, points, _ = bases.shape
    whole = lambda a: pl.BlockSpec(a.shape, lambda i, *_: (0,) * a.ndim)
    grid_spec = pltpu.PrefetchScalarGridSpec(
        num_scalar_prefetch=2,
        grid=(points // TILE,),
        in_specs=[whole(a) for a in incoming]
        + [whole(a) for a in weights]
        + [
            whole(noise),
            pl.BlockSpec((levels, TILE, R), lambda i, *_: (0, i, 0)),
            pl.BlockSpec((TILE, R), lambda i, *_: (i, 0)),
        ],
        out_specs=[
            pl.BlockSpec((points, R), lambda i, *_: (0, 0)),
            pl.BlockSpec((levels, R, R), lambda i, *_: (0, 0, 0)),
        ],
        scratch_shapes=[
            pltpu.VMEM((2 * R, R), F32),
            pltpu.VMEM((levels * R, R), BF16),
            pltpu.VMEM((levels * R, R), BF16),
            pltpu.VMEM((TILE, R), F32),
            pltpu.VMEM((R, R), F32),
            pltpu.VMEM((R, R), F32),
        ],
    )
    return pl.pallas_call(
        functools.partial(apply_kernel, levels, scales),
        grid_spec=grid_spec,
        out_shape=[
            jax.ShapeDtypeStruct((points, R), F32),
            jax.ShapeDtypeStruct((levels, R, R), F32),
        ],
        compiler_params=pltpu.CompilerParams(vmem_limit_bytes=VMEM_LIMIT),
        name="apply",
    )(order, core, *incoming, *weights, noise, bases, gathered)


def on_device(tree_order, targets, noise_var, node_bases):
    levels, points, _ = node_bases.shape
    sizes = {a: lax.axis_size(a) for a in ("y", "x", "z", "c")}
    axes = ("y", "x", "z", "c")
    plane = sizes["y"] * sizes["x"]
    all_points = points * plane * sizes["z"] * sizes["c"]
    scales = [float(all_points / 2**k) ** -0.5 for k in range(levels)]
    order = tree_order[0]
    core = lax.axis_index("c").astype(jnp.int32).reshape(1)
    noise = noise_var.reshape(points // R, R)

    def swap(value, z_bit, c_bit):
        count = plane * sizes["z"] * sizes["c"]
        flip = z_bit * sizes["c"] + c_bit
        return lax.ppermute(value, axes, [(i, i ^ flip) for i in range(count)])

    gathered, keep, give = grams(order, core, targets, noise, node_bases, scales)
    mine = keep + swap(give, 0, 1)
    parts = lax.all_to_all(mine.reshape(plane, -1, R), ("y", "x"), 0, 0)
    parts = lax.all_to_all(sum_and_copy(parts), ("y", "x"), 0, 0)
    mine = parts.reshape(-1, R)
    incoming = (mine, swap(mine, 0, 1))
    weights = []
    for level in range(levels - 1, 0, -1):
        found, left, give = solve_level(level, core, incoming)
        weights.insert(0, found)
        came = swap(give, 1 << (levels - 1 - level), 0)
        incoming = (left, came, swap(came, 0, 1))
    solved, node_weights = apply(
        order, core, incoming, weights, noise, node_bases, gathered, scales
    )
    return solved, node_weights


def solution(mesh):
    fine = Mesh(mesh.devices.reshape(4, 4, 8, 2), ("y", "x", "z", "c"))
    points = ("z", "c", "y", "x")
    in_specs = (P(points, None), P(points, None), P(points), P(None, points, None))
    out_specs = (P(points, None), P(("z", "c"), None, None))
    return jax.shard_map(
        on_device, mesh=fine, in_specs=in_specs, out_specs=out_specs, check_vma=False
    )
```

```python
import functools

import jax
import jax.numpy as jnp
from jax import lax
from jax.experimental import pallas as pl
from jax.experimental.pallas import tpu as pltpu
from jax.sharding import Mesh, PartitionSpec as P

R = 128
TILE = 1024
F32 = jnp.float32
BF16 = jnp.bfloat16
MIB = 1024 * 1024


def three(a):
    a1 = a.astype(BF16)
    rest = a - a1.astype(F32)
    a2 = rest.astype(BF16)
    return a1, a2, (rest - a2.astype(F32)).astype(BF16)


def left3(a):
    a1, a2 = split(a)
    return jnp.concatenate([a1, a1, a2], axis=1)


def right3(b):
    b1, b2 = split(b)
    return jnp.concatenate([b1, b2, b1], axis=0)


def left6(a):
    a1, a2, a3 = three(a)
    return jnp.concatenate([a1, a1, a2, a1, a3, a2], axis=1)


def right6(b):
    b1, b2, b3 = three(b)
    return jnp.concatenate([b1, b2, b1, b3, b1, b2], axis=0)


def dot3(a, b):
    return dot16(left3(a), right3(b))


def dot(a, b):
    return dot16(left6(a), right6(b))


def dot16(a, b):
    return jnp.dot(a, b, preferred_element_type=F32)


def dot16_t(a, b):
    return lax.dot_general(a, b, (((0,), (0,)), ((), ())), preferred_element_type=F32)


def split(a):
    high = a.astype(BF16)
    return high, (a - high.astype(F32)).astype(BF16)


def column(rows):
    parts = [
        jnp.broadcast_to(rows[i : i + 1, :], (R, R)).T for i in range(rows.shape[0])
    ]
    return jnp.concatenate(parts, axis=0)


def block(i):
    return pl.ds(i * R, R)


def block_list(levels):
    return [(k, c) for k in range(levels - 1, -1, -1) for c in range(-1, k + 1)]


def gram_kernel(levels, scales, order, core, targets, noise, bases,
                keep, give, acc, acc_t, whole, gathered):
    step = pl.program_id(0)
    tile = bases.shape[1]
    width = levels * R

    @pl.when(step == 0)
    def _():
        acc[...] = jnp.zeros_like(acc)
        acc_t[...] = jnp.zeros_like(acc_t)

    for row in range(tile):
        gathered[pl.ds(row, 1), :] = targets[pl.ds(order[step * tile + row], 1), :]
    root = column(1.0 / jnp.sqrt(noise[pl.ds(step * (tile // R), tile // R), :]))
    pieces = [split(bases[k] * root) for k in range(levels)]
    high = jnp.concatenate([p[0] for p in pieces], axis=1)
    low = jnp.concatenate([p[1] for p in pieces], axis=1)
    right_h, right_l = split(gathered[...] * root)
    turned = high.T
    every = jnp.concatenate([high, low, right_h, right_l], axis=1)
    near = width // 2
    acc[0:near, 0:near] += dot16(turned[0:near, :], high[:, 0:near])
    acc[:, near:] += dot16(turned, every[:, near:])
    acc_t[...] += dot16(right_h.T, low)

    @pl.when(step == pl.num_programs(0) - 1)
    def _():
        blocks = block_list(levels)
        half = len(blocks) // 2
        for at, (k, c) in enumerate(blocks):
            rows = block(k)
            if c < 0:
                value = (
                    acc[rows, block(2 * levels)]
                    + acc[rows, block(2 * levels + 1)]
                    + acc_t[:, block(k)].T
                ) * scales[k]
            else:
                same = acc[rows, block(c)]
                if c < levels // 2 <= k:
                    same = acc[block(c), rows].T
                value = (
                    same
                    + acc[rows, block(levels + c)]
                    + acc[block(c), block(levels + k)].T
                ) * (scales[k] * scales[c])
            whole[block(at), :] = value
        rows = half * R

        @pl.when(core[0] == 0)
        def _():
            keep[...] = whole[0:rows, :]
            give[...] = whole[rows : 2 * rows, :]

        @pl.when(core[0] != 0)
        def _():
            give[...] = whole[0:rows, :]
            keep[...] = whole[rows : 2 * rows, :]


def grams(order, core, targets, noise, bases, scales):
    levels, points, _ = bases.shape
    half = len(block_list(levels)) // 2 * R
    width = levels * R
    grid_spec = pltpu.PrefetchScalarGridSpec(
        num_scalar_prefetch=2,
        grid=(points // TILE,),
        in_specs=[
            pl.BlockSpec((points, R), lambda i, *_: (0, 0)),
            pl.BlockSpec((points // R, R), lambda i, *_: (0, 0)),
            pl.BlockSpec((levels, TILE, R), lambda i, *_: (0, i, 0)),
        ],
        out_specs=[
            pl.BlockSpec((half, R), lambda i, *_: (0, 0)),
            pl.BlockSpec((half, R), lambda i, *_: (0, 0)),
        ],
        scratch_shapes=[
            pltpu.VMEM((width, 2 * width + 2 * R), F32),
            pltpu.VMEM((R, width), F32),
            pltpu.VMEM((2 * half, R), F32),
            pltpu.VMEM((TILE, R), F32),
        ],
    )
    return pl.pallas_call(
        functools.partial(gram_kernel, levels, scales),
        grid_spec=grid_spec,
        out_shape=[
            jax.ShapeDtypeStruct((half, R), F32),
            jax.ShapeDtypeStruct((half, R), F32),
        ],
        compiler_params=pltpu.CompilerParams(vmem_limit_bytes=56 * MIB),
        name="grams",
    )(order, core, targets, noise, bases)


def sum_kernel(copies, parts, out):
    total = parts[0]
    for i in range(1, parts.shape[0]):
        total = total + parts[i]
    for i in range(copies):
        out[i] = total


def sum_and_copy(parts):
    return pl.pallas_call(
        functools.partial(sum_kernel, parts.shape[0]),
        out_shape=jax.ShapeDtypeStruct(parts.shape, F32),
        compiler_params=pltpu.CompilerParams(vmem_limit_bytes=8 * MIB),
        name="sum_parts",
    )(parts)


def inverse(c, power, result):
    n = c.shape[0]
    on_diagonal = lax.broadcasted_iota(jnp.int32, (n, n), 0) == lax.broadcasted_iota(
        jnp.int32, (n, n), 1
    )
    eye = jnp.where(on_diagonal, 1.0, 0.0).astype(F32)
    diagonal = jnp.sum(c * eye, axis=0, keepdims=True)
    radius = jnp.sum(jnp.abs(c), axis=0, keepdims=True) - jnp.abs(diagonal)
    top = jnp.max(diagonal + radius)
    low = jnp.maximum(jnp.min(diagonal - radius), 1.0)
    factor = 2.0 / (low + top)
    bound = (top - low) / (low + top)
    power[...] = eye - factor * c
    result[...] = factor * (eye + power[...])

    def cond(bound):
        return bound > 1e-4

    def body(bound):
        e = dot3(power[...], power[...])
        power[...] = e
        result[...] += dot3(result[...], e)
        return bound * bound

    lax.while_loop(cond, body, bound * bound)

    def cond_r(state):
        return jnp.logical_and(state[0] > 1e-4, state[1] < 8)

    def body_r(state):
        x = result[...]
        residual = eye - dot(c, x)
        result[...] = x + dot3(x, residual)
        return jnp.max(jnp.abs(residual)), state[1] + 1

    lax.while_loop(cond_r, body_r, (jnp.float32(1.0), jnp.int32(0)))
    return result[...]


def capacitance(own):
    n = own.shape[0]
    on_diagonal = lax.broadcasted_iota(jnp.int32, (n, n), 0) == lax.broadcasted_iota(
        jnp.int32, (n, n), 1
    )
    return jnp.where(on_diagonal, 1.0, 0.0).astype(F32) + 0.5 * (own + own.T)


def eliminate(level, total, weights, left, give, core, power, result):
    get = lambda i: total[block(i), :]
    inv = left6(inverse(capacitance(get(level + 1)), power, result))
    found = []
    for i in range(level + 1):
        value = dot16(inv, right6(get(i)))
        weights[i] = value
        found.append(right6(value))
    for i, (k, col) in enumerate(block_list(level)):
        if col < 0:
            turned = left6(get(k + 1).T)
        left[block(i), :] = get(level + 2 + i) - dot16(turned, found[col + 1])
    if give is None:
        return
    size = give.shape[0]

    @pl.when(core[0] == 0)
    def _():
        give[...] = left[0:size, :]

    @pl.when(core[0] != 0)
    def _():
        give[...] = left[size : 2 * size, :]


def join(core, total, mine, other, before=None):
    half = mine.shape[0]
    for first in (0, 1):

        @pl.when(core[0] == first)
        def _():
            for place, part in ((first * half, mine), ((1 - first) * half, other)):
                value = part[...]
                if before is not None:
                    value = value + before[place : place + half, :]
                total[place : place + half, :] = value


def level_kernel(level, first, core, *refs):
    refs = list(refs)
    before = None if first else refs.pop(0)
    mine, other, weights, left, *give, total, power, result = refs
    join(core, total, mine, other, before)
    eliminate(level, total, weights, left, give[0] if give else None, core, power, result)


def solve_level(level, core, incoming):
    first = len(incoming) == 2
    after = len(block_list(level))
    smem = pl.BlockSpec(memory_space=pltpu.SMEM)
    vmem = pl.BlockSpec(memory_space=pltpu.VMEM)
    rows = 2 * incoming[-1].shape[0]
    shapes = [(level + 1, R, R), (after * R, R)]
    if level > 1:
        shapes.append((after * R // 2, R))
    return pl.pallas_call(
        functools.partial(level_kernel, level, first),
        in_specs=[smem] + [vmem] * len(incoming),
        out_specs=[vmem] * len(shapes),
        out_shape=[jax.ShapeDtypeStruct(shape, F32) for shape in shapes],
        scratch_shapes=[pltpu.VMEM((rows, R), F32)] + [pltpu.VMEM((R, R), F32)] * 2,
        compiler_params=pltpu.CompilerParams(vmem_limit_bytes=12 * MIB),
        name="level",
    )(core, *incoming)


def moves(order, start, count, pairs):
    def some(at, _):
        for j in range(64):
            row = at * 64 + j
            to = pl.ds(order[start + row], 1)
            for source, target in pairs:
                target[to, :] = source[pl.ds(start + row, 1), :]
        return 0

    lax.fori_loop(0, count // 64, some, 0)


def place_kernel(levels, with_base, order, noise, bases, *refs):
    count = len(levels)
    if with_base:
        targets, refs = refs[0], refs[1:]
    outs, refs = refs[: 2 * count], refs[2 * count :]
    if with_base:
        base, refs = refs[0], refs[1:]
    held, placed, made, in_sem, out_sem, *refs = refs
    if with_base:
        root, spread, given, based = refs
    points = held.shape[1]
    tiles = points // TILE

    def load(t, k):
        rows = pl.ds(t * TILE, TILE)
        return pltpu.make_async_copy(
            bases.at[levels[k], rows, :], held.at[k, rows, :], in_sem.at[t, k]
        )

    def save(t, i):
        rows = pl.ds(t * TILE, TILE)
        if i == 2 * count:
            return pltpu.make_async_copy(based.at[rows, :], base.at[rows, :], out_sem.at[t, i])
        return pltpu.make_async_copy(made.at[i, rows, :], outs[i].at[rows, :], out_sem.at[t, i])

    for t in range(tiles):
        for k in range(count):
            load(t, k).start()
    if with_base:
        late = pltpu.make_async_copy(targets, given, in_sem.at[0, count])
        late.start()
    for t in range(tiles):
        rows = pl.ds(t * TILE, TILE)
        over = column(1.0 / noise[pl.ds(t * (TILE // R), TILE // R), :])
        for k in range(count):
            load(t, k).wait()
            held[k, rows, :] = held[k, rows, :] * over
        pairs = [(held.at[k], placed.at[k]) for k in range(count)]
        if with_base:
            root[rows, :] = over
            pairs.append((root, spread))
        moves(order, t * TILE, TILE, pairs)
    if with_base:
        late.wait()
    for t in range(tiles):
        rows = pl.ds(t * TILE, TILE)
        for k in range(count):
            made[2 * k, rows, :], made[2 * k + 1, rows, :] = split(placed[k, rows, :])
        if with_base:
            based[rows, :] = given[rows, :] * spread[rows, :]
        for i in range(2 * count + with_base):
            save(t, i).start()
    for t in range(tiles):
        for i in range(2 * count + with_base):
            save(t, i).wait()


def place(order, noise, bases, levels, targets=None):
    points = order.shape[0]
    count, tiles = len(levels), points // TILE
    with_base = targets is not None
    anywhere = pl.BlockSpec(memory_space=pl.ANY)
    one = pltpu.VMEM((points, R), F32)
    return pl.pallas_call(
        functools.partial(place_kernel, levels, with_base),
        in_specs=[
            pl.BlockSpec(memory_space=pltpu.SMEM),
            pl.BlockSpec(memory_space=pltpu.VMEM),
        ]
        + [anywhere] * (1 + with_base),
        out_specs=[anywhere] * (2 * count + with_base),
        out_shape=[jax.ShapeDtypeStruct((points, R), BF16)] * (2 * count)
        + [jax.ShapeDtypeStruct((points, R), F32)] * with_base,
        scratch_shapes=[
            pltpu.VMEM((count, points, R), F32),
            pltpu.VMEM((count, points, R), F32),
            pltpu.VMEM((2 * count, points, R), BF16),
            pltpu.SemaphoreType.DMA((tiles, count + 1)),
            pltpu.SemaphoreType.DMA((tiles, 2 * count + 1)),
        ]
        + [one] * (4 * with_base),
        compiler_params=pltpu.CompilerParams(vmem_limit_bytes=52 * MIB),
        cost_estimate=pl.CostEstimate(
            flops=points * R * 40, bytes_accessed=11 * MIB, transcendentals=0
        ),
        name="place",
    )(order, noise, bases, *([targets] if with_base else []))


def apply_kernel(levels, scales, left, came, *refs):
    weights, refs = refs[: levels - 1], refs[levels - 1 :]
    given, refs = refs[: 2 * levels + 1], refs[2 * levels + 1 :]
    solved, node_weights, highs, lows, base, out, coefs, power, result, in_sem, out_sem = refs
    points = base.shape[0]
    tiles = points // TILE

    def copies(t):
        rows = pl.ds(t * TILE, TILE)
        made = []
        for i, source in enumerate(given):
            if i == 2 * levels:
                target = base.at[rows, :]
            else:
                target = (highs, lows)[i % 2].at[rows, block(i // 2)]
            made.append(pltpu.make_async_copy(source.at[rows, :], target, in_sem.at[t, i]))
        return made

    def write(t):
        rows = pl.ds(t * TILE, TILE)
        return pltpu.make_async_copy(out.at[rows, :], solved.at[rows, :], out_sem.at[t])

    for t in range(tiles):
        for copy in copies(t):
            copy.start()
    total = left[...] + came[...]
    inv = inverse(capacitance(total[R:, :]), power, result)
    found = [dot(inv, total[:R, :])]
    node_weights[0] = found[0]
    for k in range(1, levels):
        w = weights[k - 1]
        value = w[0]
        node_weights[k] = value
        for j in range(k):
            value = value - dot(w[j + 1], found[j])
        found.append(value)
    for k in range(levels):
        h, l = split(found[k] * scales[k])
        coefs[block(k), 0:R] = h
        coefs[block(k), R : 2 * R] = l
    for t in range(tiles):
        rows = pl.ds(t * TILE, TILE)
        for copy in copies(t):
            copy.wait()
        both = dot16(highs[rows, :], coefs[...])
        small = both[:, R : 2 * R] + dot16(lows[rows, :], coefs[:, 0:R])
        out[rows, :] = base[rows, :] - (both[:, 0:R] + small)
        write(t).start()
    for t in range(tiles):
        write(t).wait()


def apply(incoming, weights, placed, base, scales):
    points = base.shape[0]
    levels = len(scales)
    tiles = points // TILE
    vmem = pl.BlockSpec(memory_space=pltpu.VMEM)
    anywhere = pl.BlockSpec(memory_space=pl.ANY)
    return pl.pallas_call(
        functools.partial(apply_kernel, levels, scales),
        in_specs=[vmem] * (len(incoming) + len(weights)) + [anywhere] * (len(placed) + 1),
        out_specs=[anywhere, vmem],
        out_shape=[
            jax.ShapeDtypeStruct((points, R), F32),
            jax.ShapeDtypeStruct((levels, R, R), F32),
        ],
        scratch_shapes=[
            pltpu.VMEM((points, levels * R), BF16),
            pltpu.VMEM((points, levels * R), BF16),
            pltpu.VMEM((points, R), F32),
            pltpu.VMEM((points, R), F32),
            pltpu.VMEM((levels * R, 2 * R), BF16),
            pltpu.VMEM((R, R), F32),
            pltpu.VMEM((R, R), F32),
            pltpu.SemaphoreType.DMA((tiles, 2 * levels + 1)),
            pltpu.SemaphoreType.DMA((tiles,)),
        ],
        compiler_params=pltpu.CompilerParams(vmem_limit_bytes=52 * MIB),
        name="apply",
    )(*incoming, *weights, *placed, base)


def on_device(tree_order, targets, noise_var, node_bases):
    levels, points, _ = node_bases.shape
    sizes = {a: lax.axis_size(a) for a in ("y", "x", "z", "c")}
    axes = ("y", "x", "z", "c")
    plane = sizes["y"] * sizes["x"]
    all_points = points * plane * sizes["z"] * sizes["c"]
    scales = [float(all_points / 2**k) ** -0.5 for k in range(levels)]
    order = tree_order[0]
    core = lax.axis_index("c").astype(jnp.int32).reshape(1)
    noise = noise_var.reshape(points // R, R)

    def swap(value, z_bit, c_bit):
        count = plane * sizes["z"] * sizes["c"]
        flip = z_bit * sizes["c"] + c_bit
        return lax.ppermute(value, axes, [(i, i ^ flip) for i in range(count)])

    keep, give = grams(order, core, targets, noise, node_bases, scales)
    mine = keep + swap(give, 0, 1)

    def beside(value, move, picked, extra=None):
        value, when = lax.optimization_barrier((value, order))
        value = move(value)
        made = place(when, noise, node_bases, picked, extra)
        value, *made = lax.optimization_barrier((value, *made))
        return value, made

    spread = lambda a: lax.all_to_all(a, ("y", "x"), 0, 0)
    half = levels // 2
    parts, (*placed, base) = beside(
        mine.reshape(plane, -1, R), spread, list(range(half)), targets
    )
    parts, more = beside(sum_and_copy(parts), spread, list(range(half, levels)))
    placed += more
    mine = parts.reshape(-1, R)
    incoming = (mine, swap(mine, 0, 1))
    weights = []
    for level in range(levels - 1, 0, -1):
        found, left, *give = solve_level(level, core, incoming)
        weights.insert(0, found)
        if give:
            came = swap(give[0], 1 << (levels - 1 - level), 0)
            incoming = (left, came, swap(came, 0, 1))
    came = swap(left, sizes["z"] - 1, 0)
    return tuple(apply((left, came), weights, placed, base, scales))


def solution(mesh):
    fine = Mesh(mesh.devices.reshape(4, 4, 8, 2), ("y", "x", "z", "c"))
    points = ("z", "c", "y", "x")
    in_specs = (P(points, None), P(points, None), P(points), P(None, points, None))
    out_specs = (P(points, None), P(("z", "c"), None, None))
    return jax.shard_map(
        on_device, mesh=fine, in_specs=in_specs, out_specs=out_specs, check_vma=False
    )
```

```python
import functools

import jax
import jax.numpy as jnp
from jax import lax
from jax.experimental import pallas as pl
from jax.experimental.pallas import tpu as pltpu
from jax.sharding import Mesh, PartitionSpec as P

R = 128
TILE = 1024
F32 = jnp.float32
BF16 = jnp.bfloat16
MIB = 1024 * 1024


def three(a):
    a1 = a.astype(BF16)
    rest = a - a1.astype(F32)
    a2 = rest.astype(BF16)
    return a1, a2, (rest - a2.astype(F32)).astype(BF16)


def left3(a):
    a1, a2 = split(a)
    return jnp.concatenate([a1, a1, a2], axis=1)


def right3(b):
    b1, b2 = split(b)
    return jnp.concatenate([b1, b2, b1], axis=0)


def left6(a):
    a1, a2, a3 = three(a)
    return jnp.concatenate([a1, a1, a2, a1, a3, a2], axis=1)


def right6(b):
    b1, b2, b3 = three(b)
    return jnp.concatenate([b1, b2, b1, b3, b1, b2], axis=0)


def dot3(a, b):
    return dot16(left3(a), right3(b))


def dot(a, b):
    return dot16(left6(a), right6(b))


def dot16(a, b):
    return jnp.dot(a, b, preferred_element_type=F32)


def dot16_t(a, b):
    return lax.dot_general(a, b, (((0,), (0,)), ((), ())), preferred_element_type=F32)


def split(a):
    high = a.astype(BF16)
    return high, (a - high.astype(F32)).astype(BF16)


def column(rows):
    parts = [
        jnp.broadcast_to(rows[i : i + 1, :], (R, R)).T for i in range(rows.shape[0])
    ]
    return jnp.concatenate(parts, axis=0)


def block(i):
    return pl.ds(i * R, R)


def block_list(levels):
    return [(k, c) for k in range(levels - 1, -1, -1) for c in range(-1, k + 1)]


def gram_kernel(levels, scales, core, order_in, noise_in, targets, bases, keep, give,
                acc, acc_t, whole, gathered, held, given, order, noise, in_sem):
    points = given.shape[0]
    width = levels * R
    tiles = points // TILE

    def load(t, k):
        rows = pl.ds(pl.multiple_of(t * TILE, TILE), TILE)
        return pltpu.make_async_copy(
            bases.at[k, rows, :], held.at[k, rows, :], in_sem.at[t, k]
        )

    early = [
        pltpu.make_async_copy(noise_in, noise, in_sem.at[1, levels]),
        pltpu.make_async_copy(order_in, order, in_sem.at[2, levels]),
        pltpu.make_async_copy(targets, given, in_sem.at[0, levels]),
    ]
    for copy in early:
        copy.start()
    for t in range(tiles):
        for k in range(levels):
            load(t, k).start()
    acc[...] = jnp.zeros_like(acc)
    acc_t[...] = jnp.zeros_like(acc_t)
    for copy in early:
        copy.wait()

    def some(t, _):
        for k in range(levels):
            load(t, k).wait()
        rows = pl.ds(pl.multiple_of(t * TILE, TILE), TILE)
        for row in range(TILE):
            gathered[pl.ds(row, 1), :] = given[pl.ds(order[t * TILE + row], 1), :]
        lines = TILE // R
        root = column(1.0 / jnp.sqrt(noise[pl.ds(pl.multiple_of(t * lines, lines), lines), :]))
        pieces = [split(held[k, rows, :] * root) for k in range(levels)]
        high = jnp.concatenate([p[0] for p in pieces], axis=1)
        low = jnp.concatenate([p[1] for p in pieces], axis=1)
        right_h, right_l = split(gathered[...] * root)
        turned = high.T
        every = jnp.concatenate([high, low, right_h, right_l], axis=1)
        near = width // 2
        acc[0:near, 0:near] += dot16(turned[0:near, :], high[:, 0:near])
        acc[:, near:] += dot16(turned, every[:, near:])
        acc_t[...] += dot16(right_h.T, low)
        return 0

    lax.fori_loop(0, tiles, some, 0)
    blocks = block_list(levels)
    half = len(blocks) // 2
    for at, (k, c) in enumerate(blocks):
        rows = block(k)
        if c < 0:
            value = (
                acc[rows, block(2 * levels)]
                + acc[rows, block(2 * levels + 1)]
                + acc_t[:, block(k)].T
            ) * scales[k]
        else:
            same = acc[rows, block(c)]
            if c < levels // 2 <= k:
                same = acc[block(c), rows].T
            value = (
                same
                + acc[rows, block(levels + c)]
                + acc[block(c), block(levels + k)].T
            ) * (scales[k] * scales[c])
        whole[block(at), :] = value
    rows = half * R
    for first in (0, 1):

        @pl.when(core[0] == first)
        def _():
            keep[...] = whole[first * rows : (first + 1) * rows, :]
            give[...] = whole[(1 - first) * rows : (2 - first) * rows, :]


def grams(order, core, targets, noise, bases, scales):
    levels, points, _ = bases.shape
    half = len(block_list(levels)) // 2 * R
    width = levels * R
    smem = pl.BlockSpec(memory_space=pltpu.SMEM)
    vmem = pl.BlockSpec(memory_space=pltpu.VMEM)
    hbm = pl.BlockSpec(memory_space=pltpu.HBM)
    return pl.pallas_call(
        functools.partial(gram_kernel, levels, scales),
        in_specs=[smem] + [hbm] * 4,
        out_specs=[vmem, vmem],
        out_shape=[jax.ShapeDtypeStruct((half, R), F32)] * 2,
        scratch_shapes=[
            pltpu.VMEM((width, 2 * width + 2 * R), F32),
            pltpu.VMEM((R, width), F32),
            pltpu.VMEM((2 * half, R), F32),
            pltpu.VMEM((TILE, R), F32),
            pltpu.VMEM((levels, points, R), F32),
            pltpu.VMEM((points, R), F32),
            pltpu.SMEM((points,), jnp.int32),
            pltpu.VMEM((points // R, R), F32),
            pltpu.SemaphoreType.DMA((points // TILE, levels + 1)),
        ],
        compiler_params=pltpu.CompilerParams(vmem_limit_bytes=52 * MIB),
        name="grams",
    )(core, order, noise, targets, bases)


def sum_kernel(copies, parts, out):
    total = parts[0]
    for i in range(1, parts.shape[0]):
        total = total + parts[i]
    for i in range(copies):
        out[i] = total


def sum_and_copy(parts):
    return pl.pallas_call(
        functools.partial(sum_kernel, parts.shape[0]),
        out_shape=jax.ShapeDtypeStruct(parts.shape, F32),
        compiler_params=pltpu.CompilerParams(vmem_limit_bytes=8 * MIB),
        name="sum_parts",
    )(parts)


def inverse(c, power, result):
    n = c.shape[0]
    on_diagonal = lax.broadcasted_iota(jnp.int32, (n, n), 0) == lax.broadcasted_iota(
        jnp.int32, (n, n), 1
    )
    eye = jnp.where(on_diagonal, 1.0, 0.0).astype(F32)
    diagonal = jnp.sum(c * eye, axis=0, keepdims=True)
    radius = jnp.sum(jnp.abs(c), axis=0, keepdims=True) - jnp.abs(diagonal)
    top = jnp.max(diagonal + radius)
    low = jnp.maximum(jnp.min(diagonal - radius), 1.0)
    factor = 2.0 / (low + top)
    bound = (top - low) / (low + top)
    power[...] = eye - factor * c
    result[...] = factor * (eye + power[...])

    def cond(bound):
        return bound > 1e-4

    def body(bound):
        e = dot3(power[...], power[...])
        power[...] = e
        result[...] += dot3(result[...], e)
        return bound * bound

    lax.while_loop(cond, body, bound * bound)

    def cond_r(state):
        return jnp.logical_and(state[0] > 1e-4, state[1] < 8)

    def body_r(state):
        x = result[...]
        residual = eye - dot(c, x)
        result[...] = x + dot3(x, residual)
        return jnp.max(jnp.abs(residual)), state[1] + 1

    lax.while_loop(cond_r, body_r, (jnp.float32(1.0), jnp.int32(0)))
    return result[...]


def capacitance(own):
    n = own.shape[0]
    on_diagonal = lax.broadcasted_iota(jnp.int32, (n, n), 0) == lax.broadcasted_iota(
        jnp.int32, (n, n), 1
    )
    return jnp.where(on_diagonal, 1.0, 0.0).astype(F32) + 0.5 * (own + own.T)


def eliminate(level, total, weights, left, give, core, power, result):
    get = lambda i: total[block(i), :]
    inv = left6(inverse(capacitance(get(level + 1)), power, result))
    found = []
    for i in range(level + 1):
        value = dot16(inv, right6(get(i)))
        weights[i] = value
        found.append(right6(value))
    for i, (k, col) in enumerate(block_list(level)):
        if col < 0:
            turned = left6(get(k + 1).T)
        left[block(i), :] = get(level + 2 + i) - dot16(turned, found[col + 1])
    if give is None:
        return
    size = give.shape[0]

    @pl.when(core[0] == 0)
    def _():
        give[...] = left[0:size, :]

    @pl.when(core[0] != 0)
    def _():
        give[...] = left[size : 2 * size, :]


def join(core, total, mine, other, before=None):
    half = mine.shape[0]
    for first in (0, 1):

        @pl.when(core[0] == first)
        def _():
            for place, part in ((first * half, mine), ((1 - first) * half, other)):
                value = part[...]
                if before is not None:
                    value = value + before[place : place + half, :]
                total[place : place + half, :] = value


def level_kernel(level, first, core, *refs):
    refs = list(refs)
    before = None if first else refs.pop(0)
    mine, other, weights, left, *give, total, power, result = refs
    join(core, total, mine, other, before)
    eliminate(level, total, weights, left, give[0] if give else None, core, power, result)


def solve_level(level, core, incoming):
    first = len(incoming) == 2
    after = len(block_list(level))
    smem = pl.BlockSpec(memory_space=pltpu.SMEM)
    vmem = pl.BlockSpec(memory_space=pltpu.VMEM)
    rows = 2 * incoming[-1].shape[0]
    shapes = [(level + 1, R, R), (after * R, R)]
    if level > 1:
        shapes.append((after * R // 2, R))
    return pl.pallas_call(
        functools.partial(level_kernel, level, first),
        in_specs=[smem] + [vmem] * len(incoming),
        out_specs=[vmem] * len(shapes),
        out_shape=[jax.ShapeDtypeStruct(shape, F32) for shape in shapes],
        scratch_shapes=[pltpu.VMEM((rows, R), F32)] + [pltpu.VMEM((R, R), F32)] * 2,
        compiler_params=pltpu.CompilerParams(vmem_limit_bytes=12 * MIB),
        name="level",
    )(core, *incoming)


def moves(order, start, count, pairs):
    def some(at, _):
        for j in range(64):
            row = at * 64 + j
            to = pl.ds(order[start + row], 1)
            for source, target in pairs:
                target[to, :] = source[pl.ds(start + row, 1), :]
        return 0

    lax.fori_loop(0, count // 64, some, 0)


def place_kernel(levels, with_base, order_in, noise_in, bases, *refs):
    count = len(levels)
    if with_base:
        targets, refs = refs[0], refs[1:]
    outs, refs = refs[: 2 * count], refs[2 * count :]
    if with_base:
        base, refs = refs[0], refs[1:]
    if count:
        held, placed, made, *refs = refs
    if with_base:
        root, spread, given, based, *refs = refs
    order, noise, in_sem, out_sem = refs
    points = order.shape[0]
    tiles = points // TILE

    def load(t, k):
        rows = pl.ds(t * TILE, TILE)
        return pltpu.make_async_copy(
            bases.at[levels[k], rows, :], held.at[k, rows, :], in_sem.at[t, k]
        )

    def save(t, i):
        rows = pl.ds(t * TILE, TILE)
        if i == 2 * count:
            return pltpu.make_async_copy(based.at[rows, :], base.at[rows, :], out_sem.at[t, i])
        return pltpu.make_async_copy(made.at[i, rows, :], outs[i].at[rows, :], out_sem.at[t, i])

    early = [
        pltpu.make_async_copy(noise_in, noise, in_sem.at[1, count]),
        pltpu.make_async_copy(order_in, order, in_sem.at[2, count]),
    ]
    for copy in early:
        copy.start()
    for t in range(tiles):
        for k in range(count):
            load(t, k).start()
    if with_base:
        late = pltpu.make_async_copy(targets, given, in_sem.at[0, count])
        late.start()
    for copy in early:
        copy.wait()
    for t in range(tiles):
        rows = pl.ds(t * TILE, TILE)
        over = column(1.0 / noise[pl.ds(t * (TILE // R), TILE // R), :])
        for k in range(count):
            load(t, k).wait()
            held[k, rows, :] = held[k, rows, :] * over
        pairs = [(held.at[k], placed.at[k]) for k in range(count)]
        if with_base:
            root[rows, :] = over
            pairs.append((root, spread))
        moves(order, t * TILE, TILE, pairs)
    if with_base:
        late.wait()
    for t in range(tiles):
        rows = pl.ds(t * TILE, TILE)
        for k in range(count):
            made[2 * k, rows, :], made[2 * k + 1, rows, :] = split(placed[k, rows, :])
        if with_base:
            based[rows, :] = given[rows, :] * spread[rows, :]
        for i in range(2 * count + with_base):
            save(t, i).start()
    for t in range(tiles):
        for i in range(2 * count + with_base):
            save(t, i).wait()


def place(order, noise, bases, levels, targets=None):
    points = order.shape[0]
    count, tiles = len(levels), points // TILE
    with_base = targets is not None
    hbm = pl.BlockSpec(memory_space=pltpu.HBM)
    one = pltpu.VMEM((points, R), F32)
    return pl.pallas_call(
        functools.partial(place_kernel, levels, with_base),
        in_specs=[hbm] * (3 + with_base),
        out_specs=[hbm] * (2 * count + with_base),
        out_shape=[jax.ShapeDtypeStruct((points, R), BF16)] * (2 * count)
        + [jax.ShapeDtypeStruct((points, R), F32)] * with_base,
        scratch_shapes=[
            pltpu.VMEM((count, points, R), F32),
            pltpu.VMEM((count, points, R), F32),
            pltpu.VMEM((2 * count, points, R), BF16),
        ]
        * (count > 0)
        + [one] * (4 * with_base)
        + [
            pltpu.SMEM((points,), jnp.int32),
            pltpu.VMEM((points // R, R), F32),
            pltpu.SemaphoreType.DMA((tiles, count + 1)),
            pltpu.SemaphoreType.DMA((tiles, 2 * count + 1)),
        ],
        compiler_params=pltpu.CompilerParams(vmem_limit_bytes=52 * MIB),
        cost_estimate=pl.CostEstimate(
            flops=points * R * 40, bytes_accessed=11 * MIB, transcendentals=0
        ),
        name="place",
    )(order, noise, bases, *([targets] if with_base else []))


def apply_kernel(levels, scales, left, came, *refs):
    weights, refs = refs[: levels - 1], refs[levels - 1 :]
    given, refs = refs[: 2 * levels + 1], refs[2 * levels + 1 :]
    solved, node_weights, highs, lows, base, out, coefs, power, result, in_sem, out_sem = refs
    points = base.shape[0]
    tiles = points // TILE

    def copies(t):
        rows = pl.ds(t * TILE, TILE)
        made = []
        for i, source in enumerate(given):
            if i == 2 * levels:
                target = base.at[rows, :]
            else:
                target = (highs, lows)[i % 2].at[rows, block(i // 2)]
            made.append(pltpu.make_async_copy(source.at[rows, :], target, in_sem.at[t, i]))
        return made

    def write(t):
        rows = pl.ds(t * TILE, TILE)
        return pltpu.make_async_copy(out.at[rows, :], solved.at[rows, :], out_sem.at[t])

    for t in range(tiles):
        for copy in copies(t):
            copy.start()
    total = left[...] + came[...]
    inv = inverse(capacitance(total[R:, :]), power, result)
    found = [dot(inv, total[:R, :])]
    node_weights[0] = found[0]
    for k in range(1, levels):
        w = weights[k - 1]
        value = w[0]
        node_weights[k] = value
        for j in range(k):
            value = value - dot(w[j + 1], found[j])
        found.append(value)
    for k in range(levels):
        h, l = split(found[k] * scales[k])
        coefs[block(k), 0:R] = h
        coefs[block(k), R : 2 * R] = l
    for t in range(tiles):
        rows = pl.ds(t * TILE, TILE)
        for copy in copies(t):
            copy.wait()
        both = dot16(highs[rows, :], coefs[...])
        small = both[:, R : 2 * R] + dot16(lows[rows, :], coefs[:, 0:R])
        out[rows, :] = base[rows, :] - (both[:, 0:R] + small)
        write(t).start()
    for t in range(tiles):
        write(t).wait()


def apply(incoming, weights, placed, base, scales):
    points = base.shape[0]
    levels = len(scales)
    tiles = points // TILE
    vmem = pl.BlockSpec(memory_space=pltpu.VMEM)
    hbm = pl.BlockSpec(memory_space=pltpu.HBM)
    return pl.pallas_call(
        functools.partial(apply_kernel, levels, scales),
        in_specs=[vmem] * (len(incoming) + len(weights)) + [hbm] * (len(placed) + 1),
        out_specs=[hbm, vmem],
        out_shape=[
            jax.ShapeDtypeStruct((points, R), F32),
            jax.ShapeDtypeStruct((levels, R, R), F32),
        ],
        scratch_shapes=[
            pltpu.VMEM((points, levels * R), BF16),
            pltpu.VMEM((points, levels * R), BF16),
            pltpu.VMEM((points, R), F32),
            pltpu.VMEM((points, R), F32),
            pltpu.VMEM((levels * R, 2 * R), BF16),
            pltpu.VMEM((R, R), F32),
            pltpu.VMEM((R, R), F32),
            pltpu.SemaphoreType.DMA((tiles, 2 * levels + 1)),
            pltpu.SemaphoreType.DMA((tiles,)),
        ],
        compiler_params=pltpu.CompilerParams(vmem_limit_bytes=52 * MIB),
        name="apply",
    )(*incoming, *weights, *placed, base)


def on_device(tree_order, targets, noise_var, node_bases):
    levels, points, _ = node_bases.shape
    sizes = {a: lax.axis_size(a) for a in ("y", "x", "z", "c")}
    axes = ("y", "x", "z", "c")
    plane = sizes["y"] * sizes["x"]
    all_points = points * plane * sizes["z"] * sizes["c"]
    scales = [float(all_points / 2**k) ** -0.5 for k in range(levels)]
    order = tree_order[0]
    core = lax.axis_index("c").astype(jnp.int32).reshape(1)
    noise = noise_var.reshape(points // R, R)

    def swap(value, z_bit, c_bit):
        count = plane * sizes["z"] * sizes["c"]
        flip = z_bit * sizes["c"] + c_bit
        return lax.ppermute(value, axes, [(i, i ^ flip) for i in range(count)])

    keep, give = grams(order, core, targets, noise, node_bases, scales)
    mine = keep + swap(give, 0, 1)

    def beside(value, move, picked, extra=None):
        value, when = lax.optimization_barrier((value, order))
        value = move(value)
        made = place(when, noise, node_bases, picked, extra)
        value, *made = lax.optimization_barrier((value, *made))
        return value, made

    spread = lambda a: lax.all_to_all(a, ("y", "x"), 0, 0)
    half = levels // 2
    parts, placed = beside(mine.reshape(plane, -1, R), spread, list(range(half)))
    parts = spread(sum_and_copy(parts))
    mine = parts.reshape(-1, R)
    incoming = (mine, swap(mine, 0, 1))
    weights = []
    for level in range(levels - 1, 0, -1):
        found, left, *give = solve_level(level, core, incoming)
        weights.insert(0, found)
        if give:
            move = lambda a: swap(a, 1 << (levels - 1 - level), 0)
            came, more = beside(give[0], move, [half - 1 + len(weights)])
            placed += more
            incoming = (left, came, swap(came, 0, 1))
    move = lambda a: swap(a, sizes["z"] - 1, 0)
    came, (base,) = beside(left, move, [], targets)
    return tuple(apply((left, came), weights, placed, base, scales))


def solution(mesh):
    fine = Mesh(mesh.devices.reshape(4, 4, 8, 2), ("y", "x", "z", "c"))
    points = ("z", "c", "y", "x")
    in_specs = (P(points, None), P(points, None), P(points), P(None, points, None))
    out_specs = (P(points, None), P(("z", "c"), None, None))
    return jax.shard_map(
        on_device, mesh=fine, in_specs=in_specs, out_specs=out_specs, check_vma=False
    )
```

```python
import functools

import jax
import jax.numpy as jnp
from jax import lax
from jax.experimental import pallas as pl
from jax.experimental.pallas import tpu as pltpu
from jax.sharding import Mesh, PartitionSpec as P

R = 128
TILE = 1024
F32 = jnp.float32
BF16 = jnp.bfloat16
MIB = 1024 * 1024


def three(a):
    a1 = a.astype(BF16)
    rest = a - a1.astype(F32)
    a2 = rest.astype(BF16)
    return a1, a2, (rest - a2.astype(F32)).astype(BF16)


def left6(a):
    a1, a2, a3 = three(a)
    return jnp.concatenate([a1, a1, a2, a1, a3, a2], axis=1)


def right6(b):
    b1, b2, b3 = three(b)
    return jnp.concatenate([b1, b2, b1, b3, b1, b2], axis=0)


def dot(a, b):
    return dot16(left6(a), right6(b))


def dot16(a, b):
    return jnp.dot(a, b, preferred_element_type=F32)


def dot16_t(a, b):
    return lax.dot_general(a, b, (((0,), (0,)), ((), ())), preferred_element_type=F32)


def split(a):
    high = a.astype(BF16)
    return high, (a - high.astype(F32)).astype(BF16)


def column(rows):
    parts = [
        jnp.broadcast_to(rows[i : i + 1, :], (R, R)).T for i in range(rows.shape[0])
    ]
    return jnp.concatenate(parts, axis=0)


def block(i):
    return pl.ds(i * R, R)


def block_list(levels):
    return [(k, c) for k in range(levels - 1, -1, -1) for c in range(-1, k + 1)]


def gram_kernel(levels, scales, core, order_in, noise_in, targets, bases, keep, give,
                acc, acc_t, whole, gathered, held, given, order, noise, in_sem):
    points = given.shape[0]
    width = levels * R
    tiles = points // TILE

    def load(t, k):
        rows = pl.ds(pl.multiple_of(t * TILE, TILE), TILE)
        return pltpu.make_async_copy(
            bases.at[k, rows, :], held.at[k, rows, :], in_sem.at[t, k]
        )

    early = [
        pltpu.make_async_copy(noise_in, noise, in_sem.at[1, levels]),
        pltpu.make_async_copy(order_in, order, in_sem.at[2, levels]),
        pltpu.make_async_copy(targets, given, in_sem.at[0, levels]),
    ]
    for copy in early:
        copy.start()
    for t in range(tiles):
        for k in range(levels):
            load(t, k).start()
    acc[...] = jnp.zeros_like(acc)
    acc_t[...] = jnp.zeros_like(acc_t)
    for copy in early:
        copy.wait()

    def some(t, _):
        for k in range(levels):
            load(t, k).wait()
        rows = pl.ds(pl.multiple_of(t * TILE, TILE), TILE)
        for row in range(TILE):
            gathered[pl.ds(row, 1), :] = given[pl.ds(order[t * TILE + row], 1), :]
        lines = TILE // R
        root = column(1.0 / jnp.sqrt(noise[pl.ds(pl.multiple_of(t * lines, lines), lines), :]))
        pieces = [split(held[k, rows, :] * root) for k in range(levels)]
        high = jnp.concatenate([p[0] for p in pieces], axis=1)
        low = jnp.concatenate([p[1] for p in pieces], axis=1)
        right_h, right_l = split(gathered[...] * root)
        turned = high.T
        every = jnp.concatenate([high, low, right_h, right_l], axis=1)
        near = width // 2
        acc[0:near, 0:near] += dot16(turned[0:near, :], high[:, 0:near])
        acc[:, near:] += dot16(turned, every[:, near:])
        acc_t[...] += dot16(right_h.T, low)
        return 0

    lax.fori_loop(0, tiles, some, 0)
    blocks = block_list(levels)
    half = len(blocks) // 2
    for at, (k, c) in enumerate(blocks):
        rows = block(k)
        if c < 0:
            value = (
                acc[rows, block(2 * levels)]
                + acc[rows, block(2 * levels + 1)]
                + acc_t[:, block(k)].T
            ) * scales[k]
        else:
            same = acc[rows, block(c)]
            if c < levels // 2 <= k:
                same = acc[block(c), rows].T
            value = (
                same
                + acc[rows, block(levels + c)]
                + acc[block(c), block(levels + k)].T
            ) * (scales[k] * scales[c])
        whole[block(at), :] = value
    rows = half * R
    for first in (0, 1):

        @pl.when(core[0] == first)
        def _():
            keep[...] = whole[first * rows : (first + 1) * rows, :]
            give[...] = whole[(1 - first) * rows : (2 - first) * rows, :]


def grams(order, core, targets, noise, bases, scales):
    levels, points, _ = bases.shape
    half = len(block_list(levels)) // 2 * R
    width = levels * R
    smem = pl.BlockSpec(memory_space=pltpu.SMEM)
    vmem = pl.BlockSpec(memory_space=pltpu.VMEM)
    hbm = pl.BlockSpec(memory_space=pltpu.HBM)
    return pl.pallas_call(
        functools.partial(gram_kernel, levels, scales),
        in_specs=[smem] + [hbm] * 4,
        out_specs=[vmem, vmem],
        out_shape=[jax.ShapeDtypeStruct((half, R), F32)] * 2,
        scratch_shapes=[
            pltpu.VMEM((width, 2 * width + 2 * R), F32),
            pltpu.VMEM((R, width), F32),
            pltpu.VMEM((2 * half, R), F32),
            pltpu.VMEM((TILE, R), F32),
            pltpu.VMEM((levels, points, R), F32),
            pltpu.VMEM((points, R), F32),
            pltpu.SMEM((points,), jnp.int32),
            pltpu.VMEM((points // R, R), F32),
            pltpu.SemaphoreType.DMA((points // TILE, levels + 1)),
        ],
        compiler_params=pltpu.CompilerParams(vmem_limit_bytes=52 * MIB),
        name="grams",
    )(core, order, noise, targets, bases)


def sum_kernel(copies, parts, out):
    total = parts[0]
    for i in range(1, parts.shape[0]):
        total = total + parts[i]
    for i in range(copies):
        out[i] = total


def sum_and_copy(parts, copies):
    return pl.pallas_call(
        functools.partial(sum_kernel, copies),
        out_shape=jax.ShapeDtypeStruct((copies, *parts.shape[1:]), F32),
        compiler_params=pltpu.CompilerParams(vmem_limit_bytes=8 * MIB),
        name="sum_parts",
    )(parts)


def inverses(several, power, result):
    n = several[0].shape[0]
    on_diagonal = lax.broadcasted_iota(jnp.int32, (n, n), 0) == lax.broadcasted_iota(
        jnp.int32, (n, n), 1
    )
    eye = jnp.where(on_diagonal, 1.0, 0.0).astype(F32)
    bound = jnp.float32(0.0)
    for i, c in enumerate(several):
        diagonal = jnp.sum(c * eye, axis=0, keepdims=True)
        radius = jnp.sum(jnp.abs(c), axis=0, keepdims=True) - jnp.abs(diagonal)
        top = jnp.max(diagonal + radius)
        low = jnp.maximum(jnp.min(diagonal - radius), 1.0)
        factor = 2.0 / (low + top)
        bound = jnp.maximum(bound, (top - low) / (low + top))
        power[i] = eye - factor * c
        result[i] = factor * (eye + power[i])

    def cond(bound):
        return bound > 1e-4

    def body(bound):
        for i in range(len(several)):
            e = dot(power[i], power[i])
            power[i] = e
            result[i] += dot(result[i], e)
        return bound * bound

    lax.while_loop(cond, body, bound * bound)

    def cond_r(state):
        return jnp.logical_and(state[0] > 1e-4, state[1] < 8)

    def body_r(state):
        worst = jnp.float32(0.0)
        for i, c in enumerate(several):
            x = result[i]
            residual = eye - dot(c, x)
            result[i] = x + dot(x, residual)
            worst = jnp.maximum(worst, jnp.max(jnp.abs(residual)))
        return worst, state[1] + 1

    lax.while_loop(cond_r, body_r, (jnp.float32(1.0), jnp.int32(0)))
    return [result[i] for i in range(len(several))]


def capacitance(own):
    n = own.shape[0]
    on_diagonal = lax.broadcasted_iota(jnp.int32, (n, n), 0) == lax.broadcasted_iota(
        jnp.int32, (n, n), 1
    )
    return jnp.where(on_diagonal, 1.0, 0.0).astype(F32) + 0.5 * (own + own.T)


def eliminate(level, total, weights, left, give, core, power, result):
    get = lambda i: total[block(i), :]
    inv = left6(inverses([capacitance(get(level + 1))], power, result)[0])
    found = []
    for i in range(level + 1):
        value = dot16(inv, right6(get(i)))
        weights[i] = value
        found.append(right6(value))
    for i, (k, col) in enumerate(block_list(level)):
        if col < 0:
            turned = left6(get(k + 1).T)
        left[block(i), :] = get(level + 2 + i) - dot16(turned, found[col + 1])
    size = give.shape[0]

    @pl.when(core[0] == 0)
    def _():
        give[...] = left[0:size, :]

    @pl.when(core[0] != 0)
    def _():
        give[...] = left[size : 2 * size, :]


def join(core, total, mine, other, before=None):
    half = mine.shape[0]
    for first in (0, 1):

        @pl.when(core[0] == first)
        def _():
            for place, part in ((first * half, mine), ((1 - first) * half, other)):
                value = part[...]
                if before is not None:
                    value = value + before[place : place + half, :]
                total[place : place + half, :] = value


def pair_kernel(level, core, which, mine, other, weights, above, left, give,
                total, middle, power, result):
    get = lambda p, i: total[p, block(i), :]
    for p in (0, 1):
        join(core, total.at[p], mine.at[p], other.at[p])
    own = [capacitance(get(p, level + 1)) for p in (0, 1)]
    inv = [left6(x) for x in inverses(own, power, result)]
    found = [[], []]
    for i in range(level + 1):
        values = [dot16(inv[p], right6(get(p, i))) for p in (0, 1)]
        weights[i] = jnp.where(which[0] == 0, values[0], values[1])
        for p in (0, 1):
            found[p].append(right6(values[p]))
    for i, (k, col) in enumerate(block_list(level)):
        if col < 0:
            turned = [left6(get(p, k + 1).T) for p in (0, 1)]
        parts = [get(p, level + 2 + i) - dot16(turned[p], found[p][col + 1]) for p in (0, 1)]
        middle[block(i), :] = parts[0] + parts[1]
    eliminate(level - 1, middle, above, left, give, core, power, result)


def solve_pair(level, core, which, mine, other):
    after = len(block_list(level - 1)) * R
    smem = pl.BlockSpec(memory_space=pltpu.SMEM)
    vmem = pl.BlockSpec(memory_space=pltpu.VMEM)
    shapes = [(level + 1, R, R), (level, R, R), (after, R), (after // 2, R)]
    return pl.pallas_call(
        functools.partial(pair_kernel, level),
        in_specs=[smem, smem, vmem, vmem],
        out_specs=[vmem] * 4,
        out_shape=[jax.ShapeDtypeStruct(shape, F32) for shape in shapes],
        scratch_shapes=[
            pltpu.VMEM((2, 2 * mine.shape[1], R), F32),
            pltpu.VMEM((len(block_list(level)) * R, R), F32),
        ]
        + [pltpu.VMEM((2, R, R), F32)] * 2,
        compiler_params=pltpu.CompilerParams(vmem_limit_bytes=16 * MIB),
        name="pair",
    )(core, which, mine, other)


def level_kernel(level, core, before, mine, other, weights, left, give, total, power, result):
    join(core, total, mine, other, before)
    eliminate(level, total, weights, left, give, core, power, result)


def solve_level(level, core, incoming):
    after = len(block_list(level)) * R
    smem = pl.BlockSpec(memory_space=pltpu.SMEM)
    vmem = pl.BlockSpec(memory_space=pltpu.VMEM)
    shapes = [(level + 1, R, R), (after, R), (after // 2, R)]
    return pl.pallas_call(
        functools.partial(level_kernel, level),
        in_specs=[smem] + [vmem] * 3,
        out_specs=[vmem] * 3,
        out_shape=[jax.ShapeDtypeStruct(shape, F32) for shape in shapes],
        scratch_shapes=[pltpu.VMEM(incoming[0].shape, F32)] + [pltpu.VMEM((1, R, R), F32)] * 2,
        compiler_params=pltpu.CompilerParams(vmem_limit_bytes=12 * MIB),
        name="level",
    )(core, *incoming)


def moves(order, start, count, pairs):
    def some(at, _):
        for j in range(64):
            row = at * 64 + j
            to = pl.ds(order[start + row], 1)
            for source, target in pairs:
                target[to, :] = source[pl.ds(start + row, 1), :]
        return 0

    lax.fori_loop(0, count // 64, some, 0)


def place_kernel(levels, with_base, order_in, noise_in, bases, *refs):
    count = len(levels)
    if with_base:
        targets, refs = refs[0], refs[1:]
    outs, refs = refs[: 2 * count], refs[2 * count :]
    if with_base:
        base, refs = refs[0], refs[1:]
    if count:
        held, placed, made, *refs = refs
    if with_base:
        root, spread, given, based, *refs = refs
    order, noise, in_sem, out_sem = refs
    points = order.shape[0]
    tiles = points // TILE

    def load(t, k):
        rows = pl.ds(t * TILE, TILE)
        return pltpu.make_async_copy(
            bases.at[levels[k], rows, :], held.at[k, rows, :], in_sem.at[t, k]
        )

    def save(t, i):
        rows = pl.ds(t * TILE, TILE)
        if i == 2 * count:
            return pltpu.make_async_copy(based.at[rows, :], base.at[rows, :], out_sem.at[t, i])
        return pltpu.make_async_copy(made.at[i, rows, :], outs[i].at[rows, :], out_sem.at[t, i])

    early = [
        pltpu.make_async_copy(noise_in, noise, in_sem.at[1, count]),
        pltpu.make_async_copy(order_in, order, in_sem.at[2, count]),
    ]
    for copy in early:
        copy.start()
    for t in range(tiles):
        for k in range(count):
            load(t, k).start()
    if with_base:
        late = pltpu.make_async_copy(targets, given, in_sem.at[0, count])
        late.start()
    for copy in early:
        copy.wait()
    for t in range(tiles):
        rows = pl.ds(t * TILE, TILE)
        over = column(1.0 / noise[pl.ds(t * (TILE // R), TILE // R), :])
        for k in range(count):
            load(t, k).wait()
            held[k, rows, :] = held[k, rows, :] * over
        pairs = [(held.at[k], placed.at[k]) for k in range(count)]
        if with_base:
            root[rows, :] = over
            pairs.append((root, spread))
        moves(order, t * TILE, TILE, pairs)
    if with_base:
        late.wait()
    for t in range(tiles):
        rows = pl.ds(t * TILE, TILE)
        for k in range(count):
            made[2 * k, rows, :], made[2 * k + 1, rows, :] = split(placed[k, rows, :])
        if with_base:
            based[rows, :] = given[rows, :] * spread[rows, :]
        for i in range(2 * count + with_base):
            save(t, i).start()
    for t in range(tiles):
        for i in range(2 * count + with_base):
            save(t, i).wait()


def place(order, noise, bases, levels, targets=None):
    points = order.shape[0]
    count, tiles = len(levels), points // TILE
    with_base = targets is not None
    hbm = pl.BlockSpec(memory_space=pltpu.HBM)
    one = pltpu.VMEM((points, R), F32)
    return pl.pallas_call(
        functools.partial(place_kernel, levels, with_base),
        in_specs=[hbm] * (3 + with_base),
        out_specs=[hbm] * (2 * count + with_base),
        out_shape=[jax.ShapeDtypeStruct((points, R), BF16)] * (2 * count)
        + [jax.ShapeDtypeStruct((points, R), F32)] * with_base,
        scratch_shapes=[
            pltpu.VMEM((count, points, R), F32),
            pltpu.VMEM((count, points, R), F32),
            pltpu.VMEM((2 * count, points, R), BF16),
        ]
        * (count > 0)
        + [one] * (4 * with_base)
        + [
            pltpu.SMEM((points,), jnp.int32),
            pltpu.VMEM((points // R, R), F32),
            pltpu.SemaphoreType.DMA((tiles, count + 1)),
            pltpu.SemaphoreType.DMA((tiles, 2 * count + 1)),
        ],
        compiler_params=pltpu.CompilerParams(vmem_limit_bytes=52 * MIB),
        cost_estimate=pl.CostEstimate(
            flops=points * R * 40, bytes_accessed=11 * MIB, transcendentals=0
        ),
        name="place",
    )(order, noise, bases, *([targets] if with_base else []))


def chain_kernel(*refs):
    *weights, plain, slope = refs
    for k, w in enumerate(weights):
        value, factor = w[0], -w[1]
        for j in range(k):
            left = left6(w[j + 2])
            value = value - dot16(left, right6(plain[j]))
            factor = factor - dot16(left, right6(slope[j]))
        plain[k] = value
        slope[k] = factor


def chain(weights):
    count = len(weights)
    return pl.pallas_call(
        chain_kernel,
        out_shape=[jax.ShapeDtypeStruct((count, R, R), F32)] * 2,
        compiler_params=pltpu.CompilerParams(vmem_limit_bytes=8 * MIB),
        cost_estimate=pl.CostEstimate(
            flops=40 * 2 * R**3, bytes_accessed=20 * 4 * R * R, transcendentals=0
        ),
        name="chain",
    )(*weights)


def apply_kernel(levels, scales, core, before, mine, other, *refs):
    weights, (plain, slope), refs = refs[: levels - 1], refs[levels - 1 : levels + 1], refs[levels + 1 :]
    given, refs = refs[: 2 * levels + 1], refs[2 * levels + 1 :]
    solved, node_weights, highs, lows, base, out, coefs, total, power, result, *refs = refs
    in_sem, out_sem = refs
    points = base.shape[0]
    tiles = points // TILE

    def copies(t):
        rows = pl.ds(t * TILE, TILE)
        made = []
        for i, source in enumerate(given):
            if i == 2 * levels:
                target = base.at[rows, :]
            else:
                target = (highs, lows)[i % 2].at[rows, block(i // 2)]
            made.append(pltpu.make_async_copy(source.at[rows, :], target, in_sem.at[t, i]))
        return made

    def write(t):
        rows = pl.ds(t * TILE, TILE)
        return pltpu.make_async_copy(out.at[rows, :], solved.at[rows, :], out_sem.at[t])

    for t in range(tiles):
        for copy in copies(t):
            copy.start()
    join(core, total, mine, other, before)
    inv = inverses([capacitance(total[R:, :])], power, result)[0]
    root = dot(inv, total[:R, :])
    node_weights[0] = root
    found = [root]
    root = right6(root)
    for k in range(1, levels):
        node_weights[k] = weights[k - 1][0]
        found.append(plain[k - 1] + dot16(left6(slope[k - 1]), root))
    for k in range(levels):
        h, l = split(found[k] * scales[k])
        coefs[block(k), 0:R] = h
        coefs[block(k), R : 2 * R] = l
    for t in range(tiles):
        rows = pl.ds(t * TILE, TILE)
        for copy in copies(t):
            copy.wait()
        both = dot16(highs[rows, :], coefs[...])
        small = both[:, R : 2 * R] + dot16(lows[rows, :], coefs[:, 0:R])
        out[rows, :] = base[rows, :] - (both[:, 0:R] + small)
        write(t).start()
    for t in range(tiles):
        write(t).wait()


def apply(core, incoming, weights, chained, placed, base, scales):
    points = base.shape[0]
    levels = len(scales)
    tiles = points // TILE
    vmem = pl.BlockSpec(memory_space=pltpu.VMEM)
    hbm = pl.BlockSpec(memory_space=pltpu.HBM)
    return pl.pallas_call(
        functools.partial(apply_kernel, levels, scales),
        in_specs=[pl.BlockSpec(memory_space=pltpu.SMEM)]
        + [vmem] * (len(incoming) + len(weights) + 2)
        + [hbm] * (len(placed) + 1),
        out_specs=[hbm, vmem],
        out_shape=[
            jax.ShapeDtypeStruct((points, R), F32),
            jax.ShapeDtypeStruct((levels, R, R), F32),
        ],
        scratch_shapes=[
            pltpu.VMEM((points, levels * R), BF16),
            pltpu.VMEM((points, levels * R), BF16),
            pltpu.VMEM((points, R), F32),
            pltpu.VMEM((points, R), F32),
            pltpu.VMEM((levels * R, 2 * R), BF16),
            pltpu.VMEM((2 * R, R), F32),
            pltpu.VMEM((1, R, R), F32),
            pltpu.VMEM((1, R, R), F32),
            pltpu.SemaphoreType.DMA((tiles, 2 * levels + 1)),
            pltpu.SemaphoreType.DMA((tiles,)),
        ],
        compiler_params=pltpu.CompilerParams(vmem_limit_bytes=52 * MIB),
        name="apply",
    )(core, *incoming, *weights, *chained, *placed, base)


def on_device(tree_order, targets, noise_var, node_bases):
    levels, points, _ = node_bases.shape
    axes = ("y", "x", "quad", "pair", "c")
    sizes = {a: lax.axis_size(a) for a in axes}
    plane = sizes["y"] * sizes["x"]
    planes = sizes["quad"] * sizes["pair"]
    all_points = points * plane * planes * sizes["c"]
    scales = [float(all_points / 2**k) ** -0.5 for k in range(levels)]
    order = tree_order[0]
    core = lax.axis_index("c").astype(jnp.int32).reshape(1)
    which = lax.axis_index("pair").astype(jnp.int32).reshape(1)
    noise = noise_var.reshape(points // R, R)

    def swap(value, z_bit, c_bit):
        count = plane * planes * sizes["c"]
        flip = z_bit * sizes["c"] + c_bit
        return lax.ppermute(value, axes, [(i, i ^ flip) for i in range(count)])

    keep, give = grams(order, core, targets, noise, node_bases, scales)
    mine = keep + swap(give, 0, 1)

    def beside(value, move, picked, extra=None):
        value, when = lax.optimization_barrier((value, order))
        value = move(value)
        made = place(when, noise, node_bases, picked, extra)
        value, *made = lax.optimization_barrier((value, *made))
        return value, made

    half = levels // 2
    parts, placed = beside(
        mine.reshape(plane, -1, R),
        lambda a: lax.all_to_all(a, ("y", "x"), 0, 0),
        list(range(half)),
    )
    parts, more = beside(
        sum_and_copy(parts, 2 * plane),
        lambda a: lax.all_to_all(a, ("pair", "y", "x"), 0, 0),
        list(range(half, levels)),
    )
    placed += more
    mine = parts.reshape(2, -1, R)
    first, second, left, give = solve_pair(levels - 1, core, which, mine, swap(mine, 0, 1))
    came, (base,) = beside(give, lambda a: swap(a, 2, 0), [], targets)
    third, left, give = solve_level(1, core, (left, came, swap(came, 0, 1)))
    came = swap(give, planes - 1, 0)
    weights = [third, second, first]
    chained = chain(weights)
    incoming = (left, came, swap(came, 0, 1))
    return tuple(apply(core, incoming, weights, chained, placed, base, scales))


def solution(mesh):
    fine = Mesh(mesh.devices.reshape(4, 4, 4, 2, 2), ("y", "x", "quad", "pair", "c"))
    points = ("quad", "pair", "c", "y", "x")
    in_specs = (P(points, None), P(points, None), P(points), P(None, points, None))
    out_specs = (P(points, None), P(("quad", "pair", "c"), None, None))
    return jax.shard_map(
        on_device, mesh=fine, in_specs=in_specs, out_specs=out_specs, check_vma=False
    )
```

```python
import functools

import jax
import jax.numpy as jnp
from jax import lax
from jax.experimental import pallas as pl
from jax.experimental.pallas import tpu as pltpu
from jax.sharding import Mesh, PartitionSpec as P

R = 128
TILE = 1024
F32 = jnp.float32
BF16 = jnp.bfloat16
MIB = 1024 * 1024


def three(a):
    a1 = a.astype(BF16)
    rest = a - a1.astype(F32)
    a2 = rest.astype(BF16)
    return a1, a2, (rest - a2.astype(F32)).astype(BF16)


def left6(a):
    a1, a2, a3 = three(a)
    return jnp.concatenate([a1, a1, a2, a1, a3, a2], axis=1)


def right6(b):
    b1, b2, b3 = three(b)
    return jnp.concatenate([b1, b2, b1, b3, b1, b2], axis=0)


def dot(a, b):
    return dot16(left6(a), right6(b))


def dot16(a, b):
    return jnp.dot(a, b, preferred_element_type=F32)


def dot16_t(a, b):
    return lax.dot_general(a, b, (((0,), (0,)), ((), ())), preferred_element_type=F32)


def split(a):
    high = a.astype(BF16)
    return high, (a - high.astype(F32)).astype(BF16)


def column(rows):
    parts = [
        jnp.broadcast_to(rows[i : i + 1, :], (R, R)).T for i in range(rows.shape[0])
    ]
    return jnp.concatenate(parts, axis=0)


def block(i):
    return pl.ds(i * R, R)


def block_list(levels):
    return [(k, c) for k in range(levels - 1, -1, -1) for c in range(-1, k + 1)]


def gram_kernel(levels, scales, core, order_in, noise_in, targets, bases, keep, give,
                acc, acc_t, whole, gathered, held, given, order, noise, in_sem):
    points = given.shape[0]
    width = levels * R
    tiles = points // TILE

    def load(t, k):
        rows = pl.ds(pl.multiple_of(t * TILE, TILE), TILE)
        return pltpu.make_async_copy(
            bases.at[k, rows, :], held.at[k, rows, :], in_sem.at[t, k]
        )

    early = [
        pltpu.make_async_copy(noise_in, noise, in_sem.at[1, levels]),
        pltpu.make_async_copy(order_in, order, in_sem.at[2, levels]),
        pltpu.make_async_copy(targets, given, in_sem.at[0, levels]),
    ]
    for copy in early:
        copy.start()
    for t in range(tiles):
        for k in range(levels):
            load(t, k).start()
    acc[...] = jnp.zeros_like(acc)
    acc_t[...] = jnp.zeros_like(acc_t)
    for copy in early:
        copy.wait()

    def some(t, _):
        for k in range(levels):
            load(t, k).wait()
        rows = pl.ds(pl.multiple_of(t * TILE, TILE), TILE)
        for row in range(TILE):
            gathered[pl.ds(row, 1), :] = given[pl.ds(order[t * TILE + row], 1), :]
        lines = TILE // R
        root = column(1.0 / jnp.sqrt(noise[pl.ds(pl.multiple_of(t * lines, lines), lines), :]))
        pieces = [split(held[k, rows, :] * root) for k in range(levels)]
        high = jnp.concatenate([p[0] for p in pieces], axis=1)
        low = jnp.concatenate([p[1] for p in pieces], axis=1)
        right_h, right_l = split(gathered[...] * root)
        turned = high.T
        every = jnp.concatenate([high, low, right_h, right_l], axis=1)
        near = width // 2
        acc[0:near, 0:near] += dot16(turned[0:near, :], high[:, 0:near])
        acc[:, near:] += dot16(turned, every[:, near:])
        acc_t[...] += dot16(right_h.T, low)
        return 0

    lax.fori_loop(0, tiles, some, 0)
    blocks = block_list(levels)
    half = len(blocks) // 2
    for at, (k, c) in enumerate(blocks):
        rows = block(k)
        if c < 0:
            value = (
                acc[rows, block(2 * levels)]
                + acc[rows, block(2 * levels + 1)]
                + acc_t[:, block(k)].T
            ) * scales[k]
        else:
            same = acc[rows, block(c)]
            if c < levels // 2 <= k:
                same = acc[block(c), rows].T
            value = (
                same
                + acc[rows, block(levels + c)]
                + acc[block(c), block(levels + k)].T
            ) * (scales[k] * scales[c])
        whole[block(at), :] = value
    rows = half * R
    for first in (0, 1):

        @pl.when(core[0] == first)
        def _():
            keep[...] = whole[first * rows : (first + 1) * rows, :]
            give[...] = whole[(1 - first) * rows : (2 - first) * rows, :]


def grams(order, core, targets, noise, bases, scales):
    levels, points, _ = bases.shape
    half = len(block_list(levels)) // 2 * R
    width = levels * R
    smem = pl.BlockSpec(memory_space=pltpu.SMEM)
    vmem = pl.BlockSpec(memory_space=pltpu.VMEM)
    hbm = pl.BlockSpec(memory_space=pltpu.HBM)
    return pl.pallas_call(
        functools.partial(gram_kernel, levels, scales),
        in_specs=[smem] + [hbm] * 4,
        out_specs=[vmem, vmem],
        out_shape=[jax.ShapeDtypeStruct((half, R), F32)] * 2,
        scratch_shapes=[
            pltpu.VMEM((width, 2 * width + 2 * R), F32),
            pltpu.VMEM((R, width), F32),
            pltpu.VMEM((2 * half, R), F32),
            pltpu.VMEM((TILE, R), F32),
            pltpu.VMEM((levels, points, R), F32),
            pltpu.VMEM((points, R), F32),
            pltpu.SMEM((points,), jnp.int32),
            pltpu.VMEM((points // R, R), F32),
            pltpu.SemaphoreType.DMA((points // TILE, levels + 1)),
        ],
        compiler_params=pltpu.CompilerParams(vmem_limit_bytes=52 * MIB),
        name="grams",
    )(core, order, noise, targets, bases)


def sum_kernel(copies, parts, out):
    total = parts[0]
    for i in range(1, parts.shape[0]):
        total = total + parts[i]
    for i in range(copies):
        out[i] = total


def sum_and_copy(parts, copies):
    return pl.pallas_call(
        functools.partial(sum_kernel, copies),
        out_shape=jax.ShapeDtypeStruct((copies, *parts.shape[1:]), F32),
        compiler_params=pltpu.CompilerParams(vmem_limit_bytes=8 * MIB),
        name="sum_parts",
    )(parts)


def inverses(several, power, result):
    n = several[0].shape[0]
    on_diagonal = lax.broadcasted_iota(jnp.int32, (n, n), 0) == lax.broadcasted_iota(
        jnp.int32, (n, n), 1
    )
    eye = jnp.where(on_diagonal, 1.0, 0.0).astype(F32)
    bound = jnp.float32(0.0)
    for i, c in enumerate(several):
        diagonal = jnp.sum(c * eye, axis=0, keepdims=True)
        radius = jnp.sum(jnp.abs(c), axis=0, keepdims=True) - jnp.abs(diagonal)
        top = jnp.max(diagonal + radius)
        low = jnp.maximum(jnp.min(diagonal - radius), 1.0)
        factor = 2.0 / (low + top)
        bound = jnp.maximum(bound, (top - low) / (low + top))
        power[i] = eye - factor * c
        result[i] = factor * (eye + power[i])

    def cond(bound):
        return bound > 1e-4

    def body(bound):
        for i in range(len(several)):
            e = dot(power[i], power[i])
            power[i] = e
            result[i] += dot(result[i], e)
        return bound * bound

    lax.while_loop(cond, body, bound * bound)

    def cond_r(state):
        return jnp.logical_and(state[0] > 1e-4, state[1] < 8)

    def body_r(state):
        worst = jnp.float32(0.0)
        for i, c in enumerate(several):
            x = result[i]
            residual = eye - dot(c, x)
            result[i] = x + dot(x, residual)
            worst = jnp.maximum(worst, jnp.max(jnp.abs(residual)))
        return worst, state[1] + 1

    lax.while_loop(cond_r, body_r, (jnp.float32(1.0), jnp.int32(0)))
    return [result[i] for i in range(len(several))]


def capacitance(own):
    n = own.shape[0]
    on_diagonal = lax.broadcasted_iota(jnp.int32, (n, n), 0) == lax.broadcasted_iota(
        jnp.int32, (n, n), 1
    )
    return jnp.where(on_diagonal, 1.0, 0.0).astype(F32) + 0.5 * (own + own.T)


def row_of(get, count):
    return jnp.concatenate([get(i) for i in range(count)], axis=1)


def eliminate(level, total, weights, left, give, core, power, result):
    get = lambda i: total[block(i), :]
    inv = left6(inverses([capacitance(get(level + 1))], power, result)[0])
    found = dot16(inv, right6(row_of(get, level + 1)))
    for i in range(level + 1):
        weights[i] = found[:, i * R : (i + 1) * R]
    found = right6(found)
    at = 0
    for k in range(level - 1, -1, -1):
        change = dot16(left6(get(k + 1).T), found[:, : (k + 2) * R])
        for i in range(k + 2):
            left[block(at), :] = get(level + 2 + at) - change[:, i * R : (i + 1) * R]
            at += 1
    size = give.shape[0]

    @pl.when(core[0] == 0)
    def _():
        give[...] = left[0:size, :]

    @pl.when(core[0] != 0)
    def _():
        give[...] = left[size : 2 * size, :]


def join(core, total, mine, other, before=None):
    half = mine.shape[0]
    for first in (0, 1):

        @pl.when(core[0] == first)
        def _():
            for place, part in ((first * half, mine), ((1 - first) * half, other)):
                value = part[...]
                if before is not None:
                    value = value + before[place : place + half, :]
                total[place : place + half, :] = value


def pair_kernel(level, core, which, mine, other, weights, above, left, give,
                total, middle, power, result):
    get = lambda p, i: total[p, block(i), :]
    for p in (0, 1):
        join(core, total.at[p], mine.at[p], other.at[p])
    own = [capacitance(get(p, level + 1)) for p in (0, 1)]
    inv = [left6(x) for x in inverses(own, power, result)]
    found = [dot16(inv[p], right6(row_of(lambda i: get(p, i), level + 1))) for p in (0, 1)]
    for i in range(level + 1):
        cols = slice(i * R, (i + 1) * R)
        weights[i] = jnp.where(which[0] == 0, found[0][:, cols], found[1][:, cols])
    found = [right6(value) for value in found]
    at = 0
    for k in range(level - 1, -1, -1):
        change = [dot16(left6(get(p, k + 1).T), found[p][:, : (k + 2) * R]) for p in (0, 1)]
        for i in range(k + 2):
            cols = slice(i * R, (i + 1) * R)
            parts = [get(p, level + 2 + at) - change[p][:, cols] for p in (0, 1)]
            middle[block(at), :] = parts[0] + parts[1]
            at += 1
    eliminate(level - 1, middle, above, left, give, core, power, result)


def solve_pair(level, core, which, mine, other):
    after = len(block_list(level - 1)) * R
    smem = pl.BlockSpec(memory_space=pltpu.SMEM)
    vmem = pl.BlockSpec(memory_space=pltpu.VMEM)
    shapes = [(level + 1, R, R), (level, R, R), (after, R), (after // 2, R)]
    return pl.pallas_call(
        functools.partial(pair_kernel, level),
        in_specs=[smem, smem, vmem, vmem],
        out_specs=[vmem] * 4,
        out_shape=[jax.ShapeDtypeStruct(shape, F32) for shape in shapes],
        scratch_shapes=[
            pltpu.VMEM((2, 2 * mine.shape[1], R), F32),
            pltpu.VMEM((len(block_list(level)) * R, R), F32),
        ]
        + [pltpu.VMEM((2, R, R), F32)] * 2,
        compiler_params=pltpu.CompilerParams(vmem_limit_bytes=16 * MIB),
        name="pair",
    )(core, which, mine, other)


def level_kernel(level, core, before, mine, other, weights, left, give, total, power, result):
    join(core, total, mine, other, before)
    eliminate(level, total, weights, left, give, core, power, result)


def solve_level(level, core, incoming):
    after = len(block_list(level)) * R
    smem = pl.BlockSpec(memory_space=pltpu.SMEM)
    vmem = pl.BlockSpec(memory_space=pltpu.VMEM)
    shapes = [(level + 1, R, R), (after, R), (after // 2, R)]
    return pl.pallas_call(
        functools.partial(level_kernel, level),
        in_specs=[smem] + [vmem] * 3,
        out_specs=[vmem] * 3,
        out_shape=[jax.ShapeDtypeStruct(shape, F32) for shape in shapes],
        scratch_shapes=[pltpu.VMEM(incoming[0].shape, F32)] + [pltpu.VMEM((1, R, R), F32)] * 2,
        compiler_params=pltpu.CompilerParams(vmem_limit_bytes=12 * MIB),
        name="level",
    )(core, *incoming)


def moves(order, start, count, pairs):
    def some(at, _):
        for j in range(64):
            row = at * 64 + j
            to = pl.ds(order[start + row], 1)
            for source, target in pairs:
                target[to, :] = source[pl.ds(start + row, 1), :]
        return 0

    lax.fori_loop(0, count // 64, some, 0)


def place_kernel(levels, with_base, order_in, noise_in, bases, *refs):
    count = len(levels)
    if with_base:
        targets, refs = refs[0], refs[1:]
    outs, refs = refs[: 2 * count], refs[2 * count :]
    if with_base:
        base, refs = refs[0], refs[1:]
    if count:
        held, placed, made, *refs = refs
    if with_base:
        root, spread, given, based, *refs = refs
    order, noise, in_sem, out_sem = refs
    points = order.shape[0]
    tiles = points // TILE

    def load(t, k):
        rows = pl.ds(t * TILE, TILE)
        return pltpu.make_async_copy(
            bases.at[levels[k], rows, :], held.at[k, rows, :], in_sem.at[t, k]
        )

    def save(t, i):
        rows = pl.ds(t * TILE, TILE)
        if i == 2 * count:
            return pltpu.make_async_copy(based.at[rows, :], base.at[rows, :], out_sem.at[t, i])
        return pltpu.make_async_copy(made.at[i, rows, :], outs[i].at[rows, :], out_sem.at[t, i])

    early = [
        pltpu.make_async_copy(noise_in, noise, in_sem.at[1, count]),
        pltpu.make_async_copy(order_in, order, in_sem.at[2, count]),
    ]
    for copy in early:
        copy.start()
    for t in range(tiles):
        for k in range(count):
            load(t, k).start()
    if with_base:
        late = pltpu.make_async_copy(targets, given, in_sem.at[0, count])
        late.start()
    for copy in early:
        copy.wait()
    for t in range(tiles):
        rows = pl.ds(t * TILE, TILE)
        over = column(1.0 / noise[pl.ds(t * (TILE // R), TILE // R), :])
        for k in range(count):
            load(t, k).wait()
            held[k, rows, :] = held[k, rows, :] * over
        pairs = [(held.at[k], placed.at[k]) for k in range(count)]
        if with_base:
            root[rows, :] = over
            pairs.append((root, spread))
        moves(order, t * TILE, TILE, pairs)
    if with_base:
        late.wait()
    for t in range(tiles):
        rows = pl.ds(t * TILE, TILE)
        for k in range(count):
            made[2 * k, rows, :], made[2 * k + 1, rows, :] = split(placed[k, rows, :])
        if with_base:
            based[rows, :] = given[rows, :] * spread[rows, :]
        for i in range(2 * count + with_base):
            save(t, i).start()
    for t in range(tiles):
        for i in range(2 * count + with_base):
            save(t, i).wait()


def place(order, noise, bases, levels, targets=None):
    points = order.shape[0]
    count, tiles = len(levels), points // TILE
    with_base = targets is not None
    hbm = pl.BlockSpec(memory_space=pltpu.HBM)
    one = pltpu.VMEM((points, R), F32)
    return pl.pallas_call(
        functools.partial(place_kernel, levels, with_base),
        in_specs=[hbm] * (3 + with_base),
        out_specs=[hbm] * (2 * count + with_base),
        out_shape=[jax.ShapeDtypeStruct((points, R), BF16)] * (2 * count)
        + [jax.ShapeDtypeStruct((points, R), F32)] * with_base,
        scratch_shapes=[
            pltpu.VMEM((count, points, R), F32),
            pltpu.VMEM((count, points, R), F32),
            pltpu.VMEM((2 * count, points, R), BF16),
        ]
        * (count > 0)
        + [one] * (4 * with_base)
        + [
            pltpu.SMEM((points,), jnp.int32),
            pltpu.VMEM((points // R, R), F32),
            pltpu.SemaphoreType.DMA((tiles, count + 1)),
            pltpu.SemaphoreType.DMA((tiles, 2 * count + 1)),
        ],
        compiler_params=pltpu.CompilerParams(vmem_limit_bytes=52 * MIB),
        cost_estimate=pl.CostEstimate(
            flops=points * R * 40, bytes_accessed=11 * MIB, transcendentals=0
        ),
        name="place",
    )(order, noise, bases, *([targets] if with_base else []))


def chain_kernel(*refs):
    *weights, out = refs
    for k, w in enumerate(weights):
        value = jnp.concatenate([w[0], -w[1]], axis=1)
        for j in range(k):
            value = value - dot(w[j + 2], out[j])
        out[k] = value


def chain(weights):
    count = len(weights)
    return pl.pallas_call(
        chain_kernel,
        out_shape=jax.ShapeDtypeStruct((count, R, 2 * R), F32),
        compiler_params=pltpu.CompilerParams(vmem_limit_bytes=8 * MIB),
        cost_estimate=pl.CostEstimate(
            flops=40 * 2 * R**3, bytes_accessed=20 * 4 * R * R, transcendentals=0
        ),
        name="chain",
    )(*weights)


def apply_kernel(levels, scales, core, before, mine, other, *refs):
    weights, chained, refs = refs[: levels - 1], refs[levels - 1], refs[levels:]
    given, refs = refs[: 2 * levels + 1], refs[2 * levels + 1 :]
    solved, node_weights, highs, lows, base, out, coefs, total, power, result, *refs = refs
    in_sem, out_sem = refs
    points = base.shape[0]
    tiles = points // TILE

    def copies(t):
        rows = pl.ds(t * TILE, TILE)
        made = []
        for i, source in enumerate(given):
            if i == 2 * levels:
                target = base.at[rows, :]
            else:
                target = (highs, lows)[i % 2].at[rows, block(i // 2)]
            made.append(pltpu.make_async_copy(source.at[rows, :], target, in_sem.at[t, i]))
        return made

    def write(t):
        rows = pl.ds(t * TILE, TILE)
        return pltpu.make_async_copy(out.at[rows, :], solved.at[rows, :], out_sem.at[t])

    for t in range(tiles):
        for copy in copies(t):
            copy.start()
    join(core, total, mine, other, before)
    inv = inverses([capacitance(total[R:, :])], power, result)[0]
    root = dot(inv, total[:R, :])
    node_weights[0] = root
    found = [root]
    root = right6(root)
    for k in range(1, levels):
        node_weights[k] = weights[k - 1][0]
        found.append(chained[k - 1, :, :R] + dot16(left6(chained[k - 1, :, R:]), root))
    for k in range(levels):
        h, l = split(found[k] * scales[k])
        coefs[block(k), 0:R] = h
        coefs[block(k), R : 2 * R] = l
    for t in range(tiles):
        rows = pl.ds(t * TILE, TILE)
        for copy in copies(t):
            copy.wait()
        both = dot16(highs[rows, :], coefs[...])
        small = both[:, R : 2 * R] + dot16(lows[rows, :], coefs[:, 0:R])
        out[rows, :] = base[rows, :] - (both[:, 0:R] + small)
        write(t).start()
    for t in range(tiles):
        write(t).wait()


def apply(core, incoming, weights, chained, placed, base, scales):
    points = base.shape[0]
    levels = len(scales)
    tiles = points // TILE
    vmem = pl.BlockSpec(memory_space=pltpu.VMEM)
    hbm = pl.BlockSpec(memory_space=pltpu.HBM)
    return pl.pallas_call(
        functools.partial(apply_kernel, levels, scales),
        in_specs=[pl.BlockSpec(memory_space=pltpu.SMEM)]
        + [vmem] * (len(incoming) + len(weights) + 1)
        + [hbm] * (len(placed) + 1),
        out_specs=[hbm, vmem],
        out_shape=[
            jax.ShapeDtypeStruct((points, R), F32),
            jax.ShapeDtypeStruct((levels, R, R), F32),
        ],
        scratch_shapes=[
            pltpu.VMEM((points, levels * R), BF16),
            pltpu.VMEM((points, levels * R), BF16),
            pltpu.VMEM((points, R), F32),
            pltpu.VMEM((points, R), F32),
            pltpu.VMEM((levels * R, 2 * R), BF16),
            pltpu.VMEM((2 * R, R), F32),
            pltpu.VMEM((1, R, R), F32),
            pltpu.VMEM((1, R, R), F32),
            pltpu.SemaphoreType.DMA((tiles, 2 * levels + 1)),
            pltpu.SemaphoreType.DMA((tiles,)),
        ],
        compiler_params=pltpu.CompilerParams(vmem_limit_bytes=52 * MIB),
        name="apply",
    )(core, *incoming, *weights, chained, *placed, base)


def on_device(tree_order, targets, noise_var, node_bases):
    levels, points, _ = node_bases.shape
    axes = ("y", "x", "quad", "pair", "c")
    sizes = {a: lax.axis_size(a) for a in axes}
    plane = sizes["y"] * sizes["x"]
    planes = sizes["quad"] * sizes["pair"]
    all_points = points * plane * planes * sizes["c"]
    scales = [float(all_points / 2**k) ** -0.5 for k in range(levels)]
    order = tree_order[0]
    core = lax.axis_index("c").astype(jnp.int32).reshape(1)
    which = lax.axis_index("pair").astype(jnp.int32).reshape(1)
    noise = noise_var.reshape(points // R, R)

    def swap(value, z_bit, c_bit):
        count = plane * planes * sizes["c"]
        flip = z_bit * sizes["c"] + c_bit
        return lax.ppermute(value, axes, [(i, i ^ flip) for i in range(count)])

    keep, give = grams(order, core, targets, noise, node_bases, scales)
    mine = keep + swap(give, 0, 1)

    def beside(value, move, picked, extra=None):
        value, when = lax.optimization_barrier((value, order))
        value = move(value)
        made = place(when, noise, node_bases, picked, extra)
        value, *made = lax.optimization_barrier((value, *made))
        return value, made

    half = levels // 2
    parts, placed = beside(
        mine.reshape(plane, -1, R),
        lambda a: lax.all_to_all(a, ("y", "x"), 0, 0),
        list(range(half)),
    )
    parts, more = beside(
        sum_and_copy(parts, 2 * plane),
        lambda a: lax.all_to_all(a, ("pair", "y", "x"), 0, 0),
        list(range(half, levels)),
    )
    placed += more
    mine = parts.reshape(2, -1, R)
    first, second, left, give = solve_pair(levels - 1, core, which, mine, swap(mine, 0, 1))
    came, (base,) = beside(give, lambda a: swap(a, 2, 0), [], targets)
    third, left, give = solve_level(1, core, (left, came, swap(came, 0, 1)))
    came = swap(give, planes - 1, 0)
    weights = [third, second, first]
    chained = chain(weights)
    incoming = (left, came, swap(came, 0, 1))
    return tuple(apply(core, incoming, weights, chained, placed, base, scales))


def solution(mesh):
    fine = Mesh(mesh.devices.reshape(4, 4, 4, 2, 2), ("y", "x", "quad", "pair", "c"))
    points = ("quad", "pair", "c", "y", "x")
    in_specs = (P(points, None), P(points, None), P(points), P(None, points, None))
    out_specs = (P(points, None), P(("quad", "pair", "c"), None, None))
    return jax.shard_map(
        on_device, mesh=fine, in_specs=in_specs, out_specs=out_specs, check_vma=False
    )
```

```python
import functools

import jax
import jax.numpy as jnp
from jax import lax
from jax.experimental import pallas as pl
from jax.experimental.pallas import tpu as pltpu
from jax.sharding import Mesh, PartitionSpec as P

R = 128
TILE = 1024
F32 = jnp.float32
BF16 = jnp.bfloat16
MIB = 1024 * 1024


def three(a):
    a1 = a.astype(BF16)
    rest = a - a1.astype(F32)
    a2 = rest.astype(BF16)
    return a1, a2, (rest - a2.astype(F32)).astype(BF16)


def left6(a):
    a1, a2, a3 = three(a)
    return jnp.concatenate([a1, a1, a2, a1, a3, a2], axis=1)


def right6(b):
    b1, b2, b3 = three(b)
    return jnp.concatenate([b1, b2, b1, b3, b1, b2], axis=0)


def dot(a, b):
    return dot16(left6(a), right6(b))


def dot16(a, b):
    return jnp.dot(a, b, preferred_element_type=F32)


def dot16_t(a, b):
    return lax.dot_general(a, b, (((0,), (0,)), ((), ())), preferred_element_type=F32)


def split(a):
    high = a.astype(BF16)
    return high, (a - high.astype(F32)).astype(BF16)


def column(rows):
    parts = [
        jnp.broadcast_to(rows[i : i + 1, :], (R, R)).T for i in range(rows.shape[0])
    ]
    return jnp.concatenate(parts, axis=0)


def block(i):
    return pl.ds(i * R, R)


def block_list(levels):
    return [(k, c) for k in range(levels - 1, -1, -1) for c in range(-1, k + 1)]


def gram_kernel(levels, scales, core, order_in, noise_in, targets, bases, keep, give,
                acc, acc_t, whole, gathered, held, given, order, noise, in_sem):
    points = given.shape[0]
    width = levels * R
    tiles = points // TILE

    def load(t, k):
        rows = pl.ds(pl.multiple_of(t * TILE, TILE), TILE)
        return pltpu.make_async_copy(
            bases.at[k, rows, :], held.at[k, rows, :], in_sem.at[t, k]
        )

    early = [
        pltpu.make_async_copy(noise_in, noise, in_sem.at[1, levels]),
        pltpu.make_async_copy(order_in, order, in_sem.at[2, levels]),
        pltpu.make_async_copy(targets, given, in_sem.at[0, levels]),
    ]
    for copy in early:
        copy.start()
    for t in range(tiles):
        for k in range(levels):
            load(t, k).start()
    acc[...] = jnp.zeros_like(acc)
    acc_t[...] = jnp.zeros_like(acc_t)
    for copy in early:
        copy.wait()

    def some(t, _):
        for k in range(levels):
            load(t, k).wait()
        rows = pl.ds(pl.multiple_of(t * TILE, TILE), TILE)
        for row in range(TILE):
            gathered[pl.ds(row, 1), :] = given[pl.ds(order[t * TILE + row], 1), :]
        lines = TILE // R
        root = column(1.0 / jnp.sqrt(noise[pl.ds(pl.multiple_of(t * lines, lines), lines), :]))
        pieces = [split(held[k, rows, :] * root) for k in range(levels)]
        high = jnp.concatenate([p[0] for p in pieces], axis=1)
        low = jnp.concatenate([p[1] for p in pieces], axis=1)
        right_h, right_l = split(gathered[...] * root)
        turned = high.T
        every = jnp.concatenate([high, low, right_h, right_l], axis=1)
        near = width // 2
        acc[0:near, 0:near] += dot16(turned[0:near, :], high[:, 0:near])
        acc[:, near:] += dot16(turned, every[:, near:])
        acc_t[...] += dot16(right_h.T, low)
        return 0

    lax.fori_loop(0, tiles, some, 0)
    blocks = block_list(levels)
    half = len(blocks) // 2
    for at, (k, c) in enumerate(blocks):
        rows = block(k)
        if c < 0:
            value = (
                acc[rows, block(2 * levels)]
                + acc[rows, block(2 * levels + 1)]
                + acc_t[:, block(k)].T
            ) * scales[k]
        else:
            same = acc[rows, block(c)]
            if c < levels // 2 <= k:
                same = acc[block(c), rows].T
            value = (
                same
                + acc[rows, block(levels + c)]
                + acc[block(c), block(levels + k)].T
            ) * (scales[k] * scales[c])
        whole[block(at), :] = value
    rows = half * R
    for first in (0, 1):

        @pl.when(core[0] == first)
        def _():
            keep[...] = whole[first * rows : (first + 1) * rows, :]
            give[...] = whole[(1 - first) * rows : (2 - first) * rows, :]


def grams(order, core, targets, noise, bases, scales):
    levels, points, _ = bases.shape
    half = len(block_list(levels)) // 2 * R
    width = levels * R
    smem = pl.BlockSpec(memory_space=pltpu.SMEM)
    vmem = pl.BlockSpec(memory_space=pltpu.VMEM)
    hbm = pl.BlockSpec(memory_space=pltpu.HBM)
    return pl.pallas_call(
        functools.partial(gram_kernel, levels, scales),
        in_specs=[smem] + [hbm] * 4,
        out_specs=[vmem, vmem],
        out_shape=[jax.ShapeDtypeStruct((half, R), F32)] * 2,
        scratch_shapes=[
            pltpu.VMEM((width, 2 * width + 2 * R), F32),
            pltpu.VMEM((R, width), F32),
            pltpu.VMEM((2 * half, R), F32),
            pltpu.VMEM((TILE, R), F32),
            pltpu.VMEM((levels, points, R), F32),
            pltpu.VMEM((points, R), F32),
            pltpu.SMEM((points,), jnp.int32),
            pltpu.VMEM((points // R, R), F32),
            pltpu.SemaphoreType.DMA((points // TILE, levels + 1)),
        ],
        compiler_params=pltpu.CompilerParams(vmem_limit_bytes=52 * MIB),
        name="grams",
    )(core, order, noise, targets, bases)


def sum_kernel(copies, parts, out):
    total = parts[0]
    for i in range(1, parts.shape[0]):
        total = total + parts[i]
    for i in range(copies):
        out[i] = total


def sum_and_copy(parts, copies):
    return pl.pallas_call(
        functools.partial(sum_kernel, copies),
        out_shape=jax.ShapeDtypeStruct((copies, *parts.shape[1:]), F32),
        compiler_params=pltpu.CompilerParams(vmem_limit_bytes=8 * MIB),
        name="sum_parts",
    )(parts)


def inverses(several, power, result):
    n = several[0].shape[0]
    on_diagonal = lax.broadcasted_iota(jnp.int32, (n, n), 0) == lax.broadcasted_iota(
        jnp.int32, (n, n), 1
    )
    eye = jnp.where(on_diagonal, 1.0, 0.0).astype(F32)
    bound = jnp.float32(0.0)
    for i, c in enumerate(several):
        diagonal = jnp.sum(c * eye, axis=0, keepdims=True)
        radius = jnp.sum(jnp.abs(c), axis=0, keepdims=True) - jnp.abs(diagonal)
        top = jnp.max(diagonal + radius)
        low = jnp.maximum(jnp.min(diagonal - radius), 1.0)
        factor = 2.0 / (low + top)
        bound = jnp.maximum(bound, (top - low) / (low + top))
        e = eye - factor * c
        result[i] = factor * (eye + e)
        power[i] = dot(e, e)

    def cond(bound):
        return bound > 1e-4

    def body(bound):
        for i in range(len(several)):
            e, x = power[i], result[i]
            both = dot(jnp.concatenate([e, x], axis=0), e)
            power[i] = both[:n, :]
            result[i] = x + both[n:, :]
        return bound * bound

    lax.while_loop(cond, body, bound * bound)

    def cond_r(state):
        return jnp.logical_and(state[0] > 1e-4, state[1] < 8)

    def body_r(state):
        worst = jnp.float32(0.0)
        for i, c in enumerate(several):
            x = result[i]
            residual = eye - dot(c, x)
            result[i] = x + dot(x, residual)
            worst = jnp.maximum(worst, jnp.max(jnp.abs(residual)))
        return worst, state[1] + 1

    lax.while_loop(cond_r, body_r, (jnp.float32(1.0), jnp.int32(0)))
    return [result[i] for i in range(len(several))]


def capacitance(own):
    n = own.shape[0]
    on_diagonal = lax.broadcasted_iota(jnp.int32, (n, n), 0) == lax.broadcasted_iota(
        jnp.int32, (n, n), 1
    )
    return jnp.where(on_diagonal, 1.0, 0.0).astype(F32) + 0.5 * (own + own.T)


def row_of(get, count):
    return jnp.concatenate([get(i) for i in range(count)], axis=1)


def eliminate(level, total, weights, left, give, core, power, result):
    get = lambda i: total[block(i), :]
    inv = left6(inverses([capacitance(get(level + 1))], power, result)[0])
    found = dot16(inv, right6(row_of(get, level + 1)))
    for i in range(level + 1):
        weights[i] = found[:, i * R : (i + 1) * R]
    found = right6(found)
    at = 0
    for k in range(level - 1, -1, -1):
        change = dot16(left6(get(k + 1).T), found[:, : (k + 2) * R])
        for i in range(k + 2):
            left[block(at), :] = get(level + 2 + at) - change[:, i * R : (i + 1) * R]
            at += 1
    size = give.shape[0]

    @pl.when(core[0] == 0)
    def _():
        give[...] = left[0:size, :]

    @pl.when(core[0] != 0)
    def _():
        give[...] = left[size : 2 * size, :]


def join(core, total, mine, other, before=None):
    half = mine.shape[0]
    for first in (0, 1):

        @pl.when(core[0] == first)
        def _():
            for place, part in ((first * half, mine), ((1 - first) * half, other)):
                value = part[...]
                if before is not None:
                    value = value + before[place : place + half, :]
                total[place : place + half, :] = value


def pair_kernel(level, core, which, mine, other, weights, above, left, give,
                total, middle, power, result):
    get = lambda p, i: total[p, block(i), :]
    for p in (0, 1):
        join(core, total.at[p], mine.at[p], other.at[p])
    own = [capacitance(get(p, level + 1)) for p in (0, 1)]
    inv = [left6(x) for x in inverses(own, power, result)]
    found = [dot16(inv[p], right6(row_of(lambda i: get(p, i), level + 1))) for p in (0, 1)]
    for i in range(level + 1):
        cols = slice(i * R, (i + 1) * R)
        weights[i] = jnp.where(which[0] == 0, found[0][:, cols], found[1][:, cols])
    found = [right6(value) for value in found]
    at = 0
    for k in range(level - 1, -1, -1):
        change = [dot16(left6(get(p, k + 1).T), found[p][:, : (k + 2) * R]) for p in (0, 1)]
        for i in range(k + 2):
            cols = slice(i * R, (i + 1) * R)
            parts = [get(p, level + 2 + at) - change[p][:, cols] for p in (0, 1)]
            middle[block(at), :] = parts[0] + parts[1]
            at += 1
    eliminate(level - 1, middle, above, left, give, core, power, result)


def solve_pair(level, core, which, mine, other):
    after = len(block_list(level - 1)) * R
    smem = pl.BlockSpec(memory_space=pltpu.SMEM)
    vmem = pl.BlockSpec(memory_space=pltpu.VMEM)
    shapes = [(level + 1, R, R), (level, R, R), (after, R), (after // 2, R)]
    return pl.pallas_call(
        functools.partial(pair_kernel, level),
        in_specs=[smem, smem, vmem, vmem],
        out_specs=[vmem] * 4,
        out_shape=[jax.ShapeDtypeStruct(shape, F32) for shape in shapes],
        scratch_shapes=[
            pltpu.VMEM((2, 2 * mine.shape[1], R), F32),
            pltpu.VMEM((len(block_list(level)) * R, R), F32),
        ]
        + [pltpu.VMEM((2, R, R), F32)] * 2,
        compiler_params=pltpu.CompilerParams(vmem_limit_bytes=16 * MIB),
        name="pair",
    )(core, which, mine, other)


def level_kernel(level, core, before, mine, other, weights, left, give, total, power, result):
    join(core, total, mine, other, before)
    eliminate(level, total, weights, left, give, core, power, result)


def solve_level(level, core, incoming):
    after = len(block_list(level)) * R
    smem = pl.BlockSpec(memory_space=pltpu.SMEM)
    vmem = pl.BlockSpec(memory_space=pltpu.VMEM)
    shapes = [(level + 1, R, R), (after, R), (after // 2, R)]
    return pl.pallas_call(
        functools.partial(level_kernel, level),
        in_specs=[smem] + [vmem] * 3,
        out_specs=[vmem] * 3,
        out_shape=[jax.ShapeDtypeStruct(shape, F32) for shape in shapes],
        scratch_shapes=[pltpu.VMEM(incoming[0].shape, F32)] + [pltpu.VMEM((1, R, R), F32)] * 2,
        compiler_params=pltpu.CompilerParams(vmem_limit_bytes=12 * MIB),
        name="level",
    )(core, *incoming)


def moves(order, start, count, pairs):
    def some(at, _):
        for j in range(64):
            row = at * 64 + j
            to = pl.ds(order[start + row], 1)
            for source, target in pairs:
                target[to, :] = source[pl.ds(start + row, 1), :]
        return 0

    lax.fori_loop(0, count // 64, some, 0)


def place_kernel(levels, with_base, order_in, noise_in, bases, *refs):
    count = len(levels)
    if with_base:
        targets, refs = refs[0], refs[1:]
    outs, refs = refs[: 2 * count], refs[2 * count :]
    if with_base:
        base, refs = refs[0], refs[1:]
    if count:
        held, placed, made, *refs = refs
    if with_base:
        root, spread, given, based, *refs = refs
    order, noise, in_sem, out_sem = refs
    points = order.shape[0]
    tiles = points // TILE

    def load(t, k):
        rows = pl.ds(t * TILE, TILE)
        return pltpu.make_async_copy(
            bases.at[levels[k], rows, :], held.at[k, rows, :], in_sem.at[t, k]
        )

    def save(t, i):
        rows = pl.ds(t * TILE, TILE)
        if i == 2 * count:
            return pltpu.make_async_copy(based.at[rows, :], base.at[rows, :], out_sem.at[t, i])
        return pltpu.make_async_copy(made.at[i, rows, :], outs[i].at[rows, :], out_sem.at[t, i])

    early = [
        pltpu.make_async_copy(noise_in, noise, in_sem.at[1, count]),
        pltpu.make_async_copy(order_in, order, in_sem.at[2, count]),
    ]
    for copy in early:
        copy.start()
    for t in range(tiles):
        for k in range(count):
            load(t, k).start()
    if with_base:
        late = pltpu.make_async_copy(targets, given, in_sem.at[0, count])
        late.start()
    for copy in early:
        copy.wait()
    for t in range(tiles):
        rows = pl.ds(t * TILE, TILE)
        over = column(1.0 / noise[pl.ds(t * (TILE // R), TILE // R), :])
        for k in range(count):
            load(t, k).wait()
            held[k, rows, :] = held[k, rows, :] * over
        pairs = [(held.at[k], placed.at[k]) for k in range(count)]
        if with_base:
            root[rows, :] = over
            pairs.append((root, spread))
        moves(order, t * TILE, TILE, pairs)
    if with_base:
        late.wait()
    for t in range(tiles):
        rows = pl.ds(t * TILE, TILE)
        for k in range(count):
            made[2 * k, rows, :], made[2 * k + 1, rows, :] = split(placed[k, rows, :])
        if with_base:
            based[rows, :] = given[rows, :] * spread[rows, :]
        for i in range(2 * count + with_base):
            save(t, i).start()
    for t in range(tiles):
        for i in range(2 * count + with_base):
            save(t, i).wait()


def place(order, noise, bases, levels, targets=None):
    points = order.shape[0]
    count, tiles = len(levels), points // TILE
    with_base = targets is not None
    hbm = pl.BlockSpec(memory_space=pltpu.HBM)
    one = pltpu.VMEM((points, R), F32)
    return pl.pallas_call(
        functools.partial(place_kernel, levels, with_base),
        in_specs=[hbm] * (3 + with_base),
        out_specs=[hbm] * (2 * count + with_base),
        out_shape=[jax.ShapeDtypeStruct((points, R), BF16)] * (2 * count)
        + [jax.ShapeDtypeStruct((points, R), F32)] * with_base,
        scratch_shapes=[
            pltpu.VMEM((count, points, R), F32),
            pltpu.VMEM((count, points, R), F32),
            pltpu.VMEM((2 * count, points, R), BF16),
        ]
        * (count > 0)
        + [one] * (4 * with_base)
        + [
            pltpu.SMEM((points,), jnp.int32),
            pltpu.VMEM((points // R, R), F32),
            pltpu.SemaphoreType.DMA((tiles, count + 1)),
            pltpu.SemaphoreType.DMA((tiles, 2 * count + 1)),
        ],
        compiler_params=pltpu.CompilerParams(vmem_limit_bytes=52 * MIB),
        cost_estimate=pl.CostEstimate(
            flops=points * R * 40, bytes_accessed=11 * MIB, transcendentals=0
        ),
        name="place",
    )(order, noise, bases, *([targets] if with_base else []))


def chain_kernel(*refs):
    *weights, out = refs
    for k, w in enumerate(weights):
        value = jnp.concatenate([w[0], -w[1]], axis=1)
        for j in range(k):
            value = value - dot(w[j + 2], out[j])
        out[k] = value


def chain(weights):
    count = len(weights)
    return pl.pallas_call(
        chain_kernel,
        out_shape=jax.ShapeDtypeStruct((count, R, 2 * R), F32),
        compiler_params=pltpu.CompilerParams(vmem_limit_bytes=8 * MIB),
        cost_estimate=pl.CostEstimate(
            flops=40 * 2 * R**3, bytes_accessed=20 * 4 * R * R, transcendentals=0
        ),
        name="chain",
    )(*weights)


def apply_kernel(levels, scales, core, before, mine, other, *refs):
    weights, chained, refs = refs[: levels - 1], refs[levels - 1], refs[levels:]
    given, refs = refs[: 2 * levels + 1], refs[2 * levels + 1 :]
    solved, node_weights, highs, lows, base, out, coefs, total, power, result, *refs = refs
    in_sem, out_sem = refs
    points = base.shape[0]
    tiles = points // TILE

    def copies(t):
        rows = pl.ds(t * TILE, TILE)
        made = []
        for i, source in enumerate(given):
            if i == 2 * levels:
                target = base.at[rows, :]
            else:
                target = (highs, lows)[i % 2].at[rows, block(i // 2)]
            made.append(pltpu.make_async_copy(source.at[rows, :], target, in_sem.at[t, i]))
        return made

    def write(t):
        rows = pl.ds(t * TILE, TILE)
        return pltpu.make_async_copy(out.at[rows, :], solved.at[rows, :], out_sem.at[t])

    for t in range(tiles):
        for copy in copies(t):
            copy.start()
    join(core, total, mine, other, before)
    inv = inverses([capacitance(total[R:, :])], power, result)[0]
    root = dot(inv, total[:R, :])
    node_weights[0] = root
    found = [root]
    root = right6(root)
    for k in range(1, levels):
        node_weights[k] = weights[k - 1][0]
        found.append(chained[k - 1, :, :R] + dot16(left6(chained[k - 1, :, R:]), root))
    for k in range(levels):
        h, l = split(found[k] * scales[k])
        coefs[block(k), 0:R] = h
        coefs[block(k), R : 2 * R] = l
    for t in range(tiles):
        rows = pl.ds(t * TILE, TILE)
        for copy in copies(t):
            copy.wait()
        both = dot16(highs[rows, :], coefs[...])
        small = both[:, R : 2 * R] + dot16(lows[rows, :], coefs[:, 0:R])
        out[rows, :] = base[rows, :] - (both[:, 0:R] + small)
        write(t).start()
    for t in range(tiles):
        write(t).wait()


def apply(core, incoming, weights, chained, placed, base, scales):
    points = base.shape[0]
    levels = len(scales)
    tiles = points // TILE
    vmem = pl.BlockSpec(memory_space=pltpu.VMEM)
    hbm = pl.BlockSpec(memory_space=pltpu.HBM)
    return pl.pallas_call(
        functools.partial(apply_kernel, levels, scales),
        in_specs=[pl.BlockSpec(memory_space=pltpu.SMEM)]
        + [vmem] * (len(incoming) + len(weights) + 1)
        + [hbm] * (len(placed) + 1),
        out_specs=[hbm, vmem],
        out_shape=[
            jax.ShapeDtypeStruct((points, R), F32),
            jax.ShapeDtypeStruct((levels, R, R), F32),
        ],
        scratch_shapes=[
            pltpu.VMEM((points, levels * R), BF16),
            pltpu.VMEM((points, levels * R), BF16),
            pltpu.VMEM((points, R), F32),
            pltpu.VMEM((points, R), F32),
            pltpu.VMEM((levels * R, 2 * R), BF16),
            pltpu.VMEM((2 * R, R), F32),
            pltpu.VMEM((1, R, R), F32),
            pltpu.VMEM((1, R, R), F32),
            pltpu.SemaphoreType.DMA((tiles, 2 * levels + 1)),
            pltpu.SemaphoreType.DMA((tiles,)),
        ],
        compiler_params=pltpu.CompilerParams(vmem_limit_bytes=52 * MIB),
        name="apply",
    )(core, *incoming, *weights, chained, *placed, base)


def on_device(tree_order, targets, noise_var, node_bases):
    levels, points, _ = node_bases.shape
    axes = ("y", "x", "quad", "pair", "c")
    sizes = {a: lax.axis_size(a) for a in axes}
    plane = sizes["y"] * sizes["x"]
    planes = sizes["quad"] * sizes["pair"]
    all_points = points * plane * planes * sizes["c"]
    scales = [float(all_points / 2**k) ** -0.5 for k in range(levels)]
    order = tree_order[0]
    core = lax.axis_index("c").astype(jnp.int32).reshape(1)
    which = lax.axis_index("pair").astype(jnp.int32).reshape(1)
    noise = noise_var.reshape(points // R, R)

    def swap(value, z_bit, c_bit):
        count = plane * planes * sizes["c"]
        flip = z_bit * sizes["c"] + c_bit
        return lax.ppermute(value, axes, [(i, i ^ flip) for i in range(count)])

    keep, give = grams(order, core, targets, noise, node_bases, scales)
    mine = keep + swap(give, 0, 1)

    def beside(value, move, picked, extra=None):
        value, when = lax.optimization_barrier((value, order))
        value = move(value)
        made = place(when, noise, node_bases, picked, extra)
        value, *made = lax.optimization_barrier((value, *made))
        return value, made

    half = levels // 2
    parts, placed = beside(
        mine.reshape(plane, -1, R),
        lambda a: lax.all_to_all(a, ("y", "x"), 0, 0),
        list(range(half)),
    )
    parts, more = beside(
        sum_and_copy(parts, 2 * plane),
        lambda a: lax.all_to_all(a, ("pair", "y", "x"), 0, 0),
        list(range(half, levels)),
    )
    placed += more
    mine = parts.reshape(2, -1, R)
    first, second, left, give = solve_pair(levels - 1, core, which, mine, swap(mine, 0, 1))
    came, (base,) = beside(give, lambda a: swap(a, 2, 0), [], targets)
    third, left, give = solve_level(1, core, (left, came, swap(came, 0, 1)))
    came = swap(give, planes - 1, 0)
    weights = [third, second, first]
    chained = chain(weights)
    incoming = (left, came, swap(came, 0, 1))
    return tuple(apply(core, incoming, weights, chained, placed, base, scales))


def solution(mesh):
    fine = Mesh(mesh.devices.reshape(4, 4, 4, 2, 2), ("y", "x", "quad", "pair", "c"))
    points = ("quad", "pair", "c", "y", "x")
    in_specs = (P(points, None), P(points, None), P(points), P(None, points, None))
    out_specs = (P(points, None), P(("quad", "pair", "c"), None, None))
    return jax.shard_map(
        on_device, mesh=fine, in_specs=in_specs, out_specs=out_specs, check_vma=False
    )
```
